128 devices in a mesh: blk: 16 (over z, y), group: 8 (over x, core).
Axes of the slice: x: 4, y: 4, z: 4, core: 2. Of those that a mesh axis runs over, the one named last changes fastest.
Arguments:
- embeddings: bfloat16 [16, 8, 8, 128, 768], P('blk', 'group'), may hold values from -6 to 6
- cluster_ids: int32 [16, 8, 8, 128], P('blk', 'group'), may hold values from 0 to 1055, as said below
- orders: int32 [16, 8, 8, 128], P('blk', 'group'), may hold values from 0 to 131071, as said below
Outputs:
- nearest: float32 [16, 8, 8, 128], P('blk', 'group')
The draws below stay inside these ranges and needn't reach their ends.
Inputs may be any that keep to these rules, and one draw needn't show every extreme that they name: `cluster_ids`: points with equal cluster ids have the same index along the third dimension; the ids under 8 * 4 at third index g are g * 4 to g * 4 + 3 and may occur at every index of the first dimension, larger ids only at one. In each block of 128 points along the last dimension, every id under 8 * 4 occurs at most 32 times, and in every block some id occurs exactly 32 times. `orders`: all values are distinct.
All inputs are finite; a program needn't handle non-finite values.
Results may differ from the reference program's by a relative error of at most 0.0011.
Values may be sent and summed in bfloat16 or wider, within the bound.
A program may use at most 128 MiB of HBM per device.

```python
import jax
import jax.numpy as jnp
from jax import lax

D = 768
SLOT = 128
LARGE = 4
SMALL = 8
N_BLK = 16
N_GROUP = 8


def draw_cluster_ids(key, part):
    key = jax.random.fold_in(key, 1)
    first, second, third, fourth = jax.random.split(key, 4)
    capacity = SLOT // LARGE
    lead = (N_BLK, N_GROUP, N_GROUP)
    shape = (N_BLK, N_GROUP, N_GROUP, SLOT)
    top_pick = jax.random.randint(first, lead + (1,), 0, LARGE)
    counts = jax.random.randint(second, lead + (LARGE,), capacity // 2, capacity)
    cluster_iota = lax.broadcasted_iota(jnp.int32, lead + (LARGE,), 3)
    counts = jnp.where(cluster_iota == top_pick, capacity, counts)
    bounds = jnp.cumsum(counts, axis=-1)
    position = lax.broadcasted_iota(jnp.int32, shape, 3)
    label = jnp.sum((position[..., None] >= bounds[:, :, :, None, :]).astype(jnp.int32), axis=-1)
    noise = jax.random.randint(third, shape, 0, 1 << 20)
    perm = jnp.argsort(noise * SLOT + position, axis=-1, stable=True)
    label = jnp.take_along_axis(label, perm, axis=-1)
    small_pick = jax.random.randint(fourth, shape, 0, SMALL)
    owner = lax.broadcasted_iota(jnp.int32, shape, 2)
    device = lax.broadcasted_iota(jnp.int32, shape, 0)
    large_id = owner * LARGE + label
    small_id = N_GROUP * LARGE + (device * N_GROUP + owner) * SMALL + small_pick
    return jnp.where(label < LARGE, large_id, small_id).astype(jnp.int32)


def draw_orders(key, part):
    key = jax.random.fold_in(key, 2)
    total = N_BLK * N_GROUP * N_GROUP * SLOT
    ranks = jax.random.permutation(key, total)
    return ranks.reshape(N_BLK, N_GROUP, N_GROUP, SLOT).astype(jnp.int32)


def block_levels(key, shape, cuts, low, largest):
    loudness = 1.0
    for axis_at, parts in cuts:
        steps = jax.random.uniform(jax.random.fold_in(jax.random.fold_in(key, 6), axis_at), (parts,), jnp.float32, low / len(cuts), largest / len(cuts))
        loudness = loudness * jnp.repeat(jnp.exp(steps), shape[axis_at] // parts).reshape((-1,) + (1,) * (len(shape) - 1 - axis_at))
    return loudness


def centred(stream_key, dims, deviation, bound, pieces=(), dtype=jnp.bfloat16):
    entries = deviation * jax.random.normal(stream_key, dims, jnp.float32)
    if pieces:
        entries = entries * block_levels(stream_key, dims, pieces, -0.22, 0.18)
    return jnp.clip(entries, -bound, bound).astype(dtype)


def setup_inputs(seed: int = 0) -> dict:
    key_of = jax.random.split(jax.random.key(seed), 4)
    embeddings = centred(key_of[0], (N_BLK, N_GROUP, N_GROUP, SLOT, D), 1.0, 6.0, ((0, 16), (1, 8)))
    cluster_ids = draw_cluster_ids(jax.random.fold_in(key_of[3], 71), 0)
    orders = draw_orders(jax.random.fold_in(key_of[3], 71), 0)
    return {"embeddings": embeddings, "cluster_ids": cluster_ids, "orders": orders}


def normalize(embeddings):
    values = embeddings.astype(jnp.float32)
    total = lax.optimization_barrier(jnp.sum(values * values, axis=-1, keepdims=True))
    return (values * lax.rsqrt(total + 1e-06)).astype(jnp.bfloat16)

def reference(embeddings, cluster_ids, orders):
    unit = normalize(embeddings)
    width = unit.shape[-1]
    units = jnp.moveaxis(unit, 2, 0).reshape(N_GROUP, -1, width)
    idents = jnp.moveaxis(cluster_ids, 2, 0).reshape(N_GROUP, -1)
    places = jnp.moveaxis(orders, 2, 0).reshape(N_GROUP, -1)
    block = N_GROUP * SLOT

    def one_group(group_args):
        keys, kid, kord = group_args
        count = keys.shape[0] // block

        def row_block(query_args):
            query, qid, qord = query_args
            scores = lax.dot_general(query, keys, (((1,), (1,)), ((), ())), preferred_element_type=jnp.float32)
            valid = (qid[:, None] == kid[None, :]) & (kord[None, :] < qord[:, None])
            return jnp.maximum(lax.optimization_barrier(jnp.max(jnp.where(valid, scores, -1.0), axis=1)), -1.0)
        found = lax.map(row_block, (keys.reshape(count, block, width), kid.reshape(count, block), kord.reshape(count, block)))
        return found.reshape(-1)
    result = lax.map(one_group, (units, idents, places))
    result = result.reshape(N_GROUP, N_BLK, N_GROUP, SLOT)
    return jnp.moveaxis(result, 0, 2)
```

```python
import functools

import jax
import jax.numpy as jnp
from jax import lax
from jax.experimental import pallas as pl
from jax.experimental.pallas import tpu as pltpu
from jax.sharding import PartitionSpec as P

MESH = pl.DeviceIdType.MESH
F32 = jnp.float32
BF16 = jnp.bfloat16
D = 768
SLOT = 128
CAP = 32
LARGE_IDS = 32.0
NEVER = 1.0e9


def flip(value, bits):
    out = 0
    for shift in (1, 2, 4):
        bit = lax.rem(lax.div(value, shift), 2) + lax.rem(lax.div(bits, shift), 2)
        out = out + shift * lax.rem(bit, 2)
    return out


def iota(shape, dim):
    return lax.broadcasted_iota(jnp.int32, shape, dim)


def to_column(row):
    eye = iota((SLOT, SLOT), 0) == iota((SLOT, SLOT), 1)
    return jnp.sum(jnp.where(eye, jnp.broadcast_to(row, (SLOT, SLOT)), 0.0), axis=1, keepdims=True)


def to_row(column):
    eye = iota((SLOT, SLOT), 0) == iota((SLOT, SLOT), 1)
    return jnp.sum(jnp.where(eye, jnp.broadcast_to(column, (SLOT, SLOT)), 0.0), axis=0, keepdims=True)


def product(query, keys):
    return lax.dot_general(query, keys, (((1,), (1,)), ((), ())), preferred_element_type=F32)


def permutation(ids, group):
    large = ids < LARGE_IDS
    label = jnp.where(large, ids - 4.0 * group.astype(F32), 4.0)
    sub = iota((SLOT, SLOT), 0)
    lane = iota((SLOT, SLOT), 1)
    before = jnp.where((to_column(label) == label) & (sub < lane), 1.0, 0.0)
    rank = jnp.sum(before, axis=0, keepdims=True)
    dest = jnp.where(large, CAP * label + rank, 4096.0)
    subf = sub.astype(F32)
    taken = jnp.where(dest == subf, 1024.0, 0.0) + jnp.where(dest < subf, 1.0, 0.0)
    slot = iota((SLOT, 1), 0).astype(F32)
    free = slot - jnp.sum(taken, axis=1, keepdims=True)
    return jnp.where((dest == subf) | (free == jnp.where(large, -8192.0, rank)), 1.0, 0.0)


def permuted_meta(ids, orders, perm):
    id_high = jnp.floor(ids * (1.0 / 32))
    order_high = jnp.floor(orders * (1.0 / 1024))
    rest = orders - 1024.0 * order_high
    order_mid = jnp.floor(rest * (1.0 / 32))
    at = iota((8, SLOT), 0)
    parts = jnp.zeros((8, SLOT), F32)
    pieces = (id_high, ids - 32.0 * id_high, order_high, order_mid, rest - 32.0 * order_mid)
    for index, piece in enumerate(pieces):
        parts = jnp.where(at == index, jnp.broadcast_to(piece, (8, SLOT)), parts)
    moved = product(parts, perm)
    slot_ids = moved[0:1] * 32.0 + moved[1:2]
    slot_orders = moved[2:3] * 1024.0 + moved[3:4] * 32.0 + moved[4:5]
    large_orders = jnp.where(slot_ids < LARGE_IDS, slot_orders, NEVER)
    out = jnp.where(at == 0, jnp.broadcast_to(slot_ids, (8, SLOT)), jnp.broadcast_to(slot_orders, (8, SLOT)))
    return jnp.where(at == 2, jnp.broadcast_to(large_orders, (8, SLOT)), out)


def kernel(
    emb, ids_ref, orders_ref, out_ref,
    raw, send, recv, meta_send, meta_recv, perms, plane_meta, keys, key_meta, key_orders,
    best, large_in, small_best, final_send, final_recv,
    load_sem, xs, xr, xms, xmr, ps, pr, pms, pmr, fs, fr, fms, fmr, rs, rr, os, orr,
):
    b = lax.axis_index("blk")
    g = lax.axis_index("group")
    z, y = lax.div(b, 4), lax.rem(b, 4)
    x, core = lax.div(g, 2), lax.rem(g, 2)
    half = lax.div(z, 2)
    offset = lax.rem(y - z + 4, 4)
    busy = lax.rem(offset, 2) == 0
    host = lax.div(offset, 2)
    both = busy & (host == core)

    def target(c):
        return 4 * c + lax.rem(2 * core + c, 4)

    def relation(k):
        return lax.rem(3 * k, 8)

    def partner(k):
        return flip(g, relation(k))

    def load(k):
        return pltpu.make_async_copy(emb.at[partner(k)], raw.at[k], load_sem.at[k])

    def load_step(k, carry):
        load(k).start()
        return carry

    lax.fori_loop(0, 8, load_step, 0)

    barrier = pltpu.get_barrier_semaphore()

    def greet_line(k, carry):
        pl.semaphore_signal(barrier, inc=1, device_id=(b, partner(k)), device_id_type=MESH)
        return carry

    lax.fori_loop(1, 8, greet_line, 0)

    def greet_targets(c, carry):
        for h in range(2):
            @pl.when(jnp.logical_not((target(c) == b) & (core == h)))
            def _():
                pl.semaphore_signal(barrier, inc=1, device_id=(target(c), 2 * x + h), device_id_type=MESH)
        return carry

    lax.fori_loop(0, 4, greet_targets, 0)

    @pl.when(busy)
    def _():
        def greet_senders(i, carry):
            @pl.when(jnp.logical_not((i == b) & (host == core)))
            def _():
                pl.semaphore_signal(barrier, inc=1, device_id=(i, 2 * x + host), device_id_type=MESH)
            return carry

        lax.fori_loop(0, 16, greet_senders, 0)

    def prepare(k):
        load(k).wait()
        owner = partner(k)
        ids = ids_ref[pl.ds(owner, 1), :].astype(F32)
        orders = orders_ref[pl.ds(owner, 1), :].astype(F32)
        perm = permutation(ids, owner)
        perms[k] = perm
        values = raw[k].astype(F32)
        total = jnp.sum(values * values, axis=1, keepdims=True)
        unit = (values * lax.rsqrt(total + 1e-06)).astype(BF16)
        rows = jnp.dot(perm.astype(BF16), unit, preferred_element_type=F32).astype(BF16)
        return rows, permuted_meta(ids, orders, perm)

    def x_copies(k):
        to = (b, partner(k))
        return (
            pltpu.make_async_remote_copy(send.at[k], recv.at[k], xs.at[k], xr.at[k], to, MESH),
            pltpu.make_async_remote_copy(meta_send.at[k], meta_recv.at[k], xms.at[k], xmr.at[k], to, MESH),
        )

    def plane_copies(k, c):
        to = (target(c), 2 * x + half)
        rows = pl.ds(pl.multiple_of(c * CAP, CAP), CAP)
        spot = pl.ds(pl.multiple_of(b * CAP, CAP), CAP)
        return (
            pltpu.make_async_remote_copy(
                recv.at[k, rows], keys.at[k, spot], ps.at[k, c], pr.at[k], to, MESH),
            pltpu.make_async_remote_copy(
                plane_meta.at[k], key_meta.at[k, b], pms.at[k, c], pmr.at[k], to, MESH),
            pltpu.make_async_copy(recv.at[k, rows], keys.at[k, spot], pr.at[k]),
            pltpu.make_async_copy(plane_meta.at[k], key_meta.at[k, b], pmr.at[k]),
        )

    def is_self(c):
        return (target(c) == b) & (core == half)

    def send_plane(k):
        plane_meta[k] = meta_recv[k, 2:3, :]

        def piece(c, carry):
            far_rows, far_meta, near_rows, near_meta = plane_copies(k, c)

            @pl.when(jnp.logical_not(is_self(c)))
            def _():
                far_meta.start()
                far_rows.start()

            @pl.when(is_self(c))
            def _():
                near_meta.start()
                near_rows.start()

            return carry

        lax.fori_loop(0, 4, piece, 0)

    def share_copies(k):
        to = (b, 2 * x + 1 - core)
        rows = pl.ds(pl.multiple_of(core * 256, 256), 256)
        sources = pl.ds(pl.multiple_of(core * 8, 8), 8)
        return (
            pltpu.make_async_remote_copy(keys.at[k, rows], keys.at[k, rows], fs.at[k], fr.at[k], to, MESH),
            pltpu.make_async_remote_copy(
                key_meta.at[k, sources], key_meta.at[k, sources], fms.at[k], fmr.at[k], to, MESH),
        )

    def share(k):
        rows = keys.at[k, pl.ds(pl.multiple_of(core * 256, 256), 256)]
        sources = key_meta.at[k, pl.ds(pl.multiple_of(core * 8, 8), 8)]
        pltpu.make_async_copy(sources, sources, pmr.at[k]).wait()
        pltpu.make_async_copy(rows, rows, pr.at[k]).wait()
        for copy in share_copies(k):
            copy.start()

    lane_part = lax.div(iota((1, SLOT), 1), CAP)

    def compare(k):
        for copy in share_copies(k):
            copy.wait_recv()
        for u in range(4):
            merged = jnp.zeros((1, SLOT), F32)
            for j in range(4):
                shift = lax.rem(CAP * (j - z) + SLOT, SLOT)
                merged = jnp.where(lane_part == j, pltpu.roll(key_meta[k, 4 * u + j], shift, 1), merged)
            key_orders[k, u:u + 1, :] = merged
        query = keys[k, pl.ds(pl.multiple_of(core * 256, 256), 256)]
        places = jnp.concatenate(
            [to_column(key_orders[k, pl.ds(2 * core + i, 1), :]) for i in range(2)], axis=0)

        def old(j, found):
            for h in range(2):
                scores = product(query, keys[j, h * 256:(h + 1) * 256])
                for i in range(2):
                    u = 2 * h + i
                    part = scores[:, i * SLOT:(i + 1) * SLOT]
                    earlier = key_orders[j, u:u + 1, :] < places
                    found = jnp.maximum(found, jnp.where(earlier, part, -1.0))
                    other = jnp.max(jnp.where(earlier, -1.0, part), axis=0, keepdims=True)
                    best[u, pl.ds(j, 1), :] = jnp.maximum(best[u, pl.ds(j, 1), :], other)
            return found

        found = lax.fori_loop(0, k, old, jnp.full((256, SLOT), -1.0, F32))
        for h in range(2):
            scores = product(query, keys[k, h * 256:(h + 1) * 256])
            for i in range(2):
                u = 2 * h + i
                earlier = key_orders[k, u:u + 1, :] < places
                found = jnp.maximum(found, jnp.where(earlier, scores[:, i * SLOT:(i + 1) * SLOT], -1.0))
        column = jnp.max(found, axis=1, keepdims=True)
        for i in range(2):
            best[2 * core + i, pl.ds(k, 1), :] = to_row(column[i * SLOT:(i + 1) * SLOT])

    best[...] = jnp.full(best.shape, -1.0, F32)

    rows, meta = prepare(0)
    recv[0] = rows
    meta_recv[0] = meta

    greeted = 15 + jnp.where(busy, 16, 0) - jnp.where(both, 2, 0)
    pl.semaphore_wait(barrier, greeted)
    send_plane(0)

    def outgoing(k, carry):
        rows, meta = prepare(k)
        send[k] = rows
        meta_send[k] = meta
        for copy in x_copies(k):
            copy.start()
        return carry

    lax.fori_loop(1, 8, outgoing, 0)

    def pass_on(k, carry):
        for copy in x_copies(k):
            copy.wait_recv()
        send_plane(k)

        @pl.when(busy)
        def _():
            share(k - 1)

            @pl.when(k >= 2)
            def _():
                compare(k - 2)

        return carry

    lax.fori_loop(1, 8, pass_on, 0)

    def small(q, carry):
        query = jnp.concatenate([recv[2 * q], recv[2 * q + 1]], axis=0)
        labels = jnp.concatenate([to_column(meta_recv[2 * q + i, 0:1, :]) for i in range(2)], axis=0)
        labels = jnp.where(labels < LARGE_IDS, -1.0, labels)
        places = jnp.concatenate([to_column(meta_recv[2 * q + i, 1:2, :]) for i in range(2)], axis=0)

        def pair(j, found):
            scores = product(query, jnp.concatenate([recv[2 * j], recv[2 * j + 1]], axis=0))
            for i in range(2):
                match = (meta_recv[2 * j + i, 0:1, :] == labels) & (meta_recv[2 * j + i, 1:2, :] < places)
                found = jnp.maximum(found, jnp.where(match, scores[:, i * SLOT:(i + 1) * SLOT], -1.0))
            return found

        found = lax.fori_loop(0, 4, pair, jnp.full((256, SLOT), -1.0, F32))
        column = jnp.max(found, axis=1, keepdims=True)
        for i in range(2):
            small_best[pl.ds(2 * q + i, 1), :] = to_row(column[i * SLOT:(i + 1) * SLOT])
        return carry

    lax.fori_loop(0, 4, small, 0)

    def result_copies(i):
        spot = 2 * z + core
        return (
            pltpu.make_async_remote_copy(
                best.at[lax.div(i, 4)], large_in.at[spot], rs.at[i], rr.at[spot], (i, 2 * x + host), MESH),
            pltpu.make_async_copy(best.at[lax.div(i, 4)], large_in.at[spot], rr.at[spot]),
        )

    @pl.when(busy)
    def _():
        share(7)
        compare(6)
        compare(7)

        def give(i, carry):
            far, near = result_copies(i)

            @pl.when(jnp.logical_not((i == b) & (host == core)))
            def _():
                far.start()

            @pl.when((i == b) & (host == core))
            def _():
                near.start()

            return carry

        lax.fori_loop(0, 16, give, 0)

    lane_of = lax.div(iota((8, SLOT), 1), CAP)
    large = jnp.full((8, SLOT), -1.0, F32)
    for c in range(4):
        for h in range(2):
            pltpu.make_async_copy(large_in.at[2 * c + h], large_in.at[2 * c + h], rr.at[2 * c + h]).wait()
        shift = lax.rem(CAP * (c - y) + SLOT, SLOT)
        moved = pltpu.roll(jnp.maximum(large_in[2 * c], large_in[2 * c + 1]), shift, 1)
        large = jnp.where(lane_of == c, moved, large)
    for k in range(8):
        row = jnp.where(meta_recv[k, 0:1, :] < LARGE_IDS, large[k:k + 1], small_best[k:k + 1, :])
        final_send[k] = row

    def final_copy(k):
        return pltpu.make_async_remote_copy(
            final_send.at[k], final_recv.at[k], os.at[k], orr.at[k], (b, partner(k)), MESH)

    def final_start(k, carry):
        final_copy(k).start()
        return carry

    lax.fori_loop(1, 8, final_start, 0)
    final_recv[0] = final_send[0]

    def unpermute(k):
        out_ref[pl.ds(partner(k), 1), :] = jnp.sum(
            perms[k] * to_column(final_recv[k]), axis=0, keepdims=True)

    unpermute(0)

    def final_step(k, carry):
        final_copy(k).wait_recv()
        unpermute(k)
        return carry

    lax.fori_loop(1, 8, final_step, 0)

    def drain_line(k, carry):
        for copy in x_copies(k):
            copy.wait_send()
        final_copy(k).wait_send()
        return carry

    lax.fori_loop(1, 8, drain_line, 0)

    def drain_plane(k, carry):
        def piece(c, inner):
            far_rows, far_meta, _, _ = plane_copies(k, c)

            @pl.when(jnp.logical_not(is_self(c)))
            def _():
                far_rows.wait_send()
                far_meta.wait_send()

            return inner

        return lax.fori_loop(0, 4, piece, carry)

    lax.fori_loop(0, 8, drain_plane, 0)

    @pl.when(busy)
    def _():
        def drain_share(k, carry):
            for copy in share_copies(k):
                copy.wait_send()
            return carry

        lax.fori_loop(0, 8, drain_share, 0)

        def drain_result(i, carry):
            @pl.when(jnp.logical_not((i == b) & (host == core)))
            def _():
                result_copies(i)[0].wait_send()

            return carry

        lax.fori_loop(0, 16, drain_result, 0)


def shards(embeddings, cluster_ids, orders):
    dma = pltpu.SemaphoreType.DMA
    vmem = pltpu.VMEM
    out = pl.pallas_call(
        kernel,
        out_shape=jax.ShapeDtypeStruct((8, SLOT), F32),
        in_specs=[
            pl.BlockSpec(memory_space=pl.ANY),
            pl.BlockSpec(memory_space=pltpu.VMEM),
            pl.BlockSpec(memory_space=pltpu.VMEM),
        ],
        out_specs=pl.BlockSpec(memory_space=pltpu.VMEM),
        scratch_shapes=[
            vmem((8, SLOT, D), BF16),
            vmem((8, SLOT, D), BF16),
            vmem((8, SLOT, D), BF16),
            vmem((8, 8, SLOT), F32),
            vmem((8, 8, SLOT), F32),
            vmem((8, SLOT, SLOT), F32),
            vmem((8, 1, SLOT), F32),
            vmem((8, 512, D), BF16),
            vmem((8, 16, 1, SLOT), F32),
            vmem((8, 8, SLOT), F32),
            vmem((4, 8, SLOT), F32),
            vmem((8, 8, SLOT), F32),
            vmem((8, SLOT), F32),
            vmem((8, 1, SLOT), F32),
            vmem((8, 1, SLOT), F32),
            dma((8,)),
            dma((8,)), dma((8,)), dma((8,)), dma((8,)),
            dma((8, 4)), dma((8,)), dma((8, 4)), dma((8,)),
            dma((8,)), dma((8,)), dma((8,)), dma((8,)),
            dma((16,)), dma((8,)),
            dma((8,)), dma((8,)),
        ],
        compiler_params=pltpu.CompilerParams(
            collective_id=0, has_side_effects=True, vmem_limit_bytes=40 * 1024 * 1024),
    )(embeddings.reshape(8, SLOT, D), cluster_ids.reshape(8, SLOT), orders.reshape(8, SLOT))
    return out.reshape(1, 1, 8, SLOT)


def solution(mesh):
    in_specs = (
        P("blk", "group", None, None, None),
        P("blk", "group", None, None),
        P("blk", "group", None, None),
    )
    out_specs = P("blk", "group", None, None)
    return jax.shard_map(shards, mesh=mesh, in_specs=in_specs, out_specs=out_specs, check_vma=False)
```

```python
import jax
import jax.numpy as jnp
from jax import lax
from jax.experimental import pallas as pl
from jax.experimental.pallas import tpu as pltpu
from jax.sharding import PartitionSpec as P

MESH = pl.DeviceIdType.MESH
F32 = jnp.float32
BF16 = jnp.bfloat16
D = 768
SLOT = 128
CAP = 32
LARGE_IDS = 32.0
NEVER = 1.0e9
EARLY = 5
LAG = 3


def flip(value, bits):
    out = 0
    for shift in (1, 2, 4):
        bit = lax.rem(lax.div(value, shift), 2) + lax.rem(lax.div(bits, shift), 2)
        out = out + shift * lax.rem(bit, 2)
    return out


def iota(shape, dim):
    return lax.broadcasted_iota(jnp.int32, shape, dim)


def to_column(row):
    eye = iota((SLOT, SLOT), 0) == iota((SLOT, SLOT), 1)
    return jnp.sum(jnp.where(eye, jnp.broadcast_to(row, (SLOT, SLOT)), 0.0), axis=1, keepdims=True)


def to_row(column):
    eye = iota((SLOT, SLOT), 0) == iota((SLOT, SLOT), 1)
    return jnp.sum(jnp.where(eye, jnp.broadcast_to(column, (SLOT, SLOT)), 0.0), axis=0, keepdims=True)


def product(query, keys):
    return lax.dot_general(query, keys, (((1,), (1,)), ((), ())), preferred_element_type=F32)


def permutation(ids, group):
    large = ids < LARGE_IDS
    label = jnp.where(large, ids - 4.0 * group.astype(F32), 4.0)
    sub = iota((SLOT, SLOT), 0)
    lane = iota((SLOT, SLOT), 1)
    before = jnp.where((to_column(label) == label) & (sub < lane), 1.0, 0.0)
    rank = jnp.sum(before, axis=0, keepdims=True)
    dest = jnp.where(large, CAP * label + rank, 4096.0)
    subf = sub.astype(F32)
    taken = jnp.where(dest == subf, 1024.0, 0.0) + jnp.where(dest < subf, 1.0, 0.0)
    slot = iota((SLOT, 1), 0).astype(F32)
    free = slot - jnp.sum(taken, axis=1, keepdims=True)
    return jnp.where((dest == subf) | (free == jnp.where(large, -8192.0, rank)), 1.0, 0.0)


def permuted_meta(ids, orders, perm):
    id_high = jnp.floor(ids * (1.0 / 32))
    order_high = jnp.floor(orders * (1.0 / 1024))
    rest = orders - 1024.0 * order_high
    order_mid = jnp.floor(rest * (1.0 / 32))
    at = iota((8, SLOT), 0)
    parts = jnp.zeros((8, SLOT), F32)
    pieces = (id_high, ids - 32.0 * id_high, order_high, order_mid, rest - 32.0 * order_mid)
    for index, piece in enumerate(pieces):
        parts = jnp.where(at == index, jnp.broadcast_to(piece, (8, SLOT)), parts)
    moved = product(parts, perm)
    slot_ids = moved[0:1] * 32.0 + moved[1:2]
    slot_orders = moved[2:3] * 1024.0 + moved[3:4] * 32.0 + moved[4:5]
    large_orders = jnp.where(slot_ids < LARGE_IDS, slot_orders, NEVER)
    out = jnp.where(at == 0, jnp.broadcast_to(slot_ids, (8, SLOT)), jnp.broadcast_to(slot_orders, (8, SLOT)))
    return jnp.where(at == 2, jnp.broadcast_to(large_orders, (8, SLOT)), out)


def kernel(
    emb, ids_in, orders_in, out_ref,
    raw, ids_ref, orders_ref, send, recv, meta_send, meta_recv, perms, plane_meta, mid, mid_meta,
    keys, key_meta, key_orders, best, found_ref, tile_send, large_in, small_best, final_send, final_recv,
    load_sem, info_sem, xs, xr, xms, xmr, ps, pr, pms, pmr, ss, sr, sms, smr, fs, fr, fms, fmr,
    ts, tr, os, orr,
):
    b = lax.axis_index("blk")
    g = lax.axis_index("group")
    z, y = lax.div(b, 4), lax.rem(b, 4)
    x, core = lax.div(g, 2), lax.rem(g, 2)
    offset = lax.rem(y - z + 4, 4)
    busy = lax.rem(offset, 2) == 0
    host = lax.div(offset, 2)

    def relation(k):
        return lax.rem(3 * k, 8)

    def partner(k):
        return flip(g, relation(k))

    def load(k):
        return pltpu.make_async_copy(emb.at[partner(k)], raw.at[k], load_sem.at[k])

    info = (
        pltpu.make_async_copy(ids_in, ids_ref, info_sem.at[0]),
        pltpu.make_async_copy(orders_in, orders_ref, info_sem.at[1]),
    )
    for copy in info:
        copy.start()

    def load_step(k, carry):
        load(k).start()
        return carry

    lax.fori_loop(0, 8, load_step, 0)

    barrier = pltpu.get_barrier_semaphore()

    def greet(blk, group):
        pl.semaphore_signal(barrier, inc=1, device_id=(blk, group), device_id_type=MESH)

    for step in range(1, 4):
        for h in range(2):
            greet(4 * lax.rem(z + step, 4) + y, 2 * x + h)
            greet(4 * z + lax.rem(y + step, 4), 2 * x + h)
            greet(b, 2 * lax.rem(x + step, 4) + h)
    greet(b, 2 * x + 1 - core)

    def prepare(k):
        load(k).wait()
        owner = partner(k)
        ids = ids_ref[pl.ds(owner, 1), :].astype(F32)
        orders = orders_ref[pl.ds(owner, 1), :].astype(F32)
        perm = permutation(ids, owner)
        perms[k] = perm
        values = raw[k].astype(F32)
        total = jnp.sum(values * values, axis=1, keepdims=True)
        unit = (values * lax.rsqrt(total + 1e-06)).astype(BF16)
        rows = jnp.dot(perm.astype(BF16), unit, preferred_element_type=F32).astype(BF16)
        return rows, permuted_meta(ids, orders, perm)

    def block_of(k):
        return pl.ds(pl.multiple_of(k * SLOT, SLOT), SLOT)

    def x_copies(k):
        to = (b, partner(k))
        return (
            pltpu.make_async_remote_copy(send.at[k], recv.at[block_of(k)], xs.at[k], xr.at[k], to, MESH),
            pltpu.make_async_remote_copy(meta_send.at[k], meta_recv.at[k], xms.at[k], xmr.at[k], to, MESH),
        )

    def axes(k):
        odd = lax.rem(k, 2) == 1
        return odd, jnp.where(odd, z, y), jnp.where(odd, y, z)

    def device_at(odd, a, bb):
        return jnp.where(odd, 4 * a + bb, 4 * bb + a)

    def first_way(k, t):
        odd, a, bb = axes(k)
        end = lax.rem(t + 2 * core, 4)
        turned = (lax.rem(bb - end + 4, 4) == 2) & (lax.rem(a - t + 4, 2) == 1)
        return turned, device_at(odd, jnp.where(turned, a, t), jnp.where(turned, end, bb))

    def first_copies(k, t):
        odd, a, _ = axes(k)
        turned, stop = first_way(k, t)
        c = jnp.where(odd, t, lax.rem(t + 2 * core, 4))
        at = jnp.where(turned, 4, a)
        which = jnp.where(turned, 1, 0)
        rows = pl.ds(pl.multiple_of(k * SLOT + c * CAP, CAP), CAP)
        spot = pl.ds(pl.multiple_of(at * CAP, CAP), CAP)
        return (
            pltpu.make_async_remote_copy(
                recv.at[rows], mid.at[k, spot], ps.at[k, t], pr.at[k, which], (stop, g), MESH),
            pltpu.make_async_remote_copy(
                plane_meta.at[k], mid_meta.at[k, at], pms.at[k, t], pmr.at[k, which], (stop, g), MESH),
        )

    def first_near(k):
        odd, a, _ = axes(k)
        c = jnp.where(odd, a, lax.rem(a + 2 * core, 4))
        rows = pl.ds(pl.multiple_of(k * SLOT + c * CAP, CAP), CAP)
        spot = pl.ds(pl.multiple_of(a * CAP, CAP), CAP)
        return (
            pltpu.make_async_copy(recv.at[rows], mid.at[k, spot], pr.at[k, 0]),
            pltpu.make_async_copy(plane_meta.at[k], mid_meta.at[k, a], pmr.at[k, 0]),
        )

    def send_first(k):
        plane_meta[k] = meta_recv[k, 2:3, :]
        _, a, _ = axes(k)

        def piece(step, carry):
            rows, meta = first_copies(k, lax.rem(a + step, 4))
            meta.start()
            rows.start()
            return carry

        lax.fori_loop(1, 4, piece, 0)
        for copy in first_near(k):
            copy.start()

    def piece_copies(k, source, place, blk, sem):
        to = (blk, 2 * x + lax.div(place, 8))
        rows = pl.ds(pl.multiple_of(source * CAP, CAP), CAP)
        spot = pl.ds(pl.multiple_of(place * CAP, CAP), CAP)
        return (
            pltpu.make_async_remote_copy(
                mid.at[k, rows], keys.at[k, spot], ss.at[k, sem], sr.at[k], to, MESH),
            pltpu.make_async_remote_copy(
                mid_meta.at[k, source], key_meta.at[k, place], sms.at[k, sem], smr.at[k], to, MESH),
        )

    def block_copies(k):
        odd, a, bb = axes(k)
        blk = device_at(odd, a, lax.rem(a + 2 * core, 4))
        to = (blk, 2 * x + lax.div(bb, 2))
        rows = mid.at[k, pl.ds(0, SLOT)]
        spot = keys.at[k, pl.ds(pl.multiple_of(bb * SLOT, SLOT), SLOT)]
        meta = mid_meta.at[k, pl.ds(0, 4)]
        meta_spot = key_meta.at[k, pl.ds(pl.multiple_of(bb * 4, 4), 4)]
        return (
            pltpu.make_async_remote_copy(rows, spot, ss.at[k, 0], sr.at[k], to, MESH),
            pltpu.make_async_remote_copy(meta, meta_spot, sms.at[k, 0], smr.at[k], to, MESH),
            pltpu.make_async_copy(rows, spot, sr.at[k]),
            pltpu.make_async_copy(meta, meta_spot, smr.at[k]),
        )

    def second_kind(k):
        _, a, bb = axes(k)
        split = lax.rem(bb - a - 2 * core + 8, 4) == 2
        stays = busy & (host == core) & (lax.div(bb, 2) == core)
        return split, stays

    def split_copies(k, n):
        odd, a, bb = axes(k)
        source = lax.rem(a + 2 * n, 4)
        return piece_copies(k, source, 4 * bb + source, device_at(odd, a, lax.rem(a + 2 * core, 4)), n)

    def turned_copies(k):
        odd, a, bb = axes(k)
        blk = device_at(odd, lax.rem(bb + 2 * core, 4), bb)
        return piece_copies(k, 4, 4 * lax.rem(bb + 2, 4) + a, blk, 1)

    def send_second(k):
        split, stays = second_kind(k)

        @pl.when(split)
        def _():
            half_meta = mid_meta.at[k, pl.ds(0, 2)]
            half_rows = mid.at[k, pl.ds(0, 2 * CAP)]
            pltpu.make_async_copy(half_meta, half_meta, pmr.at[k, 0]).wait()
            pltpu.make_async_copy(half_rows, half_rows, pr.at[k, 0]).wait()
            for n in range(2):
                rows, meta = split_copies(k, n)
                meta.start()
                rows.start()

        @pl.when(jnp.logical_not(split))
        def _():
            all_meta = mid_meta.at[k, pl.ds(0, 4)]
            all_rows = mid.at[k, pl.ds(0, SLOT)]
            pltpu.make_async_copy(all_meta, all_meta, pmr.at[k, 0]).wait()
            pltpu.make_async_copy(all_rows, all_rows, pr.at[k, 0]).wait()
            far_rows, far_meta, near_rows, near_meta = block_copies(k)

            @pl.when(jnp.logical_not(stays))
            def _():
                far_meta.start()
                far_rows.start()

            @pl.when(stays)
            def _():
                near_meta.start()
                near_rows.start()

        @pl.when(jnp.logical_not(busy))
        def _():
            rows, meta = turned_copies(k)
            one_meta = mid_meta.at[k, 4]
            one_rows = mid.at[k, pl.ds(4 * CAP, CAP)]
            pltpu.make_async_copy(one_meta, one_meta, pmr.at[k, 1]).wait()
            pltpu.make_async_copy(one_rows, one_rows, pr.at[k, 1]).wait()
            meta.start()
            rows.start()

    def share_copies(k):
        to = (b, 2 * x + 1 - core)
        rows = pl.ds(pl.multiple_of(core * 256, 256), 256)
        sources = pl.ds(pl.multiple_of(core * 8, 8), 8)
        return (
            pltpu.make_async_remote_copy(keys.at[k, rows], keys.at[k, rows], fs.at[k], fr.at[k], to, MESH),
            pltpu.make_async_remote_copy(
                key_meta.at[k, sources], key_meta.at[k, sources], fms.at[k], fmr.at[k], to, MESH),
        )

    def share(k):
        rows = keys.at[k, pl.ds(pl.multiple_of(core * 256, 256), 256)]
        sources = key_meta.at[k, pl.ds(pl.multiple_of(core * 8, 8), 8)]
        pltpu.make_async_copy(sources, sources, smr.at[k]).wait()
        pltpu.make_async_copy(rows, rows, sr.at[k]).wait()
        for copy in share_copies(k):
            copy.start()

    lane_part = lax.div(iota((1, SLOT), 1), CAP)

    def merge_orders(k, u):
        merged = jnp.zeros((1, SLOT), F32)
        for j in range(4):
            shift = lax.rem(CAP * (j - z) + SLOT, SLOT)
            merged = jnp.where(lane_part == j, pltpu.roll(key_meta[k, 4 * u + j], shift, 1), merged)
        key_orders[k, pl.ds(u, 1), :] = merged

    def query_of(k):
        places = [to_column(key_orders[k, pl.ds(2 * core + i, 1), :]) for i in range(2)]
        return keys[k, pl.ds(pl.multiple_of(core * 256, 256), 256)], jnp.concatenate(places, axis=0)

    def against(query, places, j, found, one_way):
        for h in range(2):
            scores = product(query, keys[j, h * 256:(h + 1) * 256])
            for i in range(2):
                u = 2 * h + i
                part = scores[:, i * SLOT:(i + 1) * SLOT]
                earlier = key_orders[j, u:u + 1, :] < places
                found = jnp.maximum(found, jnp.where(earlier, part, -1.0))
                if not one_way:
                    other = jnp.max(jnp.where(earlier, -1.0, part), axis=0, keepdims=True)
                    best[u, pl.ds(j, 1), :] = jnp.maximum(best[u, pl.ds(j, 1), :], other)
        return found

    def compare_old(k):
        for i in range(2):
            merge_orders(k, 2 * core + i)
        query, places = query_of(k)
        start = jnp.full((256, SLOT), -1.0, F32)
        if isinstance(k, int):
            found = start
            for j in range(k):
                found = against(query, places, j, found, False)
            found_ref[...] = found
            return

        def two(j, found):
            return against(query, places, 2 * j + 1, against(query, places, 2 * j, found, False), False)

        found_ref[...] = lax.fori_loop(0, lax.div(k, 2), two, start)

        @pl.when(lax.rem(k, 2) == 1)
        def _():
            found_ref[...] = against(query, places, k - 1, found_ref[...], False)

    def compare_same(k):
        for copy in share_copies(k):
            copy.wait_recv()
        for i in range(2):
            merge_orders(k, 2 * (1 - core) + i)
        query, places = query_of(k)
        found = against(query, places, k, found_ref[...], True)
        column = jnp.max(found, axis=1, keepdims=True)
        for i in range(2):
            best[2 * core + i, pl.ds(k, 1), :] = to_row(column[i * SLOT:(i + 1) * SLOT])

    def take(k):
        share(k)
        if not isinstance(k, int):
            pl.when(k >= 1)(lambda: compare_same(k - 1))
        elif k >= 1:
            compare_same(k - 1)
        compare_old(k)

    best[...] = jnp.full(best.shape, -1.0, F32)
    for copy in info:
        copy.wait()

    rows, meta = prepare(0)
    recv[0:SLOT] = rows
    meta_recv[0] = meta

    def prepare_step(k, carry):
        rows, meta = prepare(k)
        send[k] = rows
        meta_send[k] = meta
        return carry

    def leave_step(k, carry):
        for copy in x_copies(k):
            copy.start()
        return carry

    lax.fori_loop(1, EARLY, prepare_step, 0)
    pl.semaphore_wait(barrier, 19)
    lax.fori_loop(1, EARLY, leave_step, 0)
    send_first(0)
    lax.fori_loop(EARLY, 8, lambda k, carry: leave_step(k, prepare_step(k, carry)), 0)

    def pass_on(k, carry):
        for copy in x_copies(k):
            copy.wait_recv()
        send_first(k)
        send_second(k - 1)

        @pl.when(busy & (k >= LAG))
        def _():
            take(k - LAG)

        return carry

    lax.fori_loop(1, 8, pass_on, 0)
    send_second(7)

    def small(q, carry):
        query = recv[pl.ds(pl.multiple_of(q * 256, 256), 256)]
        labels = jnp.concatenate([to_column(meta_recv[2 * q + i, 0:1, :]) for i in range(2)], axis=0)
        labels = jnp.where(labels < LARGE_IDS, -1.0, labels)
        places = jnp.concatenate([to_column(meta_recv[2 * q + i, 1:2, :]) for i in range(2)], axis=0)
        found = jnp.full((256, SLOT), -1.0, F32)
        for j in range(4):
            scores = product(query, recv[j * 256:(j + 1) * 256])
            for i in range(2):
                match = (meta_recv[2 * j + i, 0:1, :] == labels) & (meta_recv[2 * j + i, 1:2, :] < places)
                found = jnp.maximum(found, jnp.where(match, scores[:, i * SLOT:(i + 1) * SLOT], -1.0))
        column = jnp.max(found, axis=1, keepdims=True)
        for i in range(2):
            small_best[pl.ds(2 * q + i, 1), :] = to_row(column[i * SLOT:(i + 1) * SLOT])
        return carry

    lax.fori_loop(0, 4, small, 0)

    def result_copies(i):
        spot = 2 * z + core
        return (
            pltpu.make_async_remote_copy(
                tile_send.at[i], large_in.at[spot], ts.at[i], tr.at[spot], (i, 2 * x + host), MESH),
            pltpu.make_async_copy(tile_send.at[i], large_in.at[spot], tr.at[spot]),
        )

    even = lax.rem(iota((8, SLOT), 0), 2) == 0

    @pl.when(busy)
    def _():
        if LAG > 2:
            lax.fori_loop(8 - LAG, 6, lambda k, carry: (take(k), carry)[1], 0)
        take(6)
        take(7)
        compare_same(7)
        for i in range(16):
            tile_send[i] = jnp.where(even, best[i // 4], best[i % 4])
            far, near = result_copies(i)
            mine = (b == i) & (host == core)
            pl.when(jnp.logical_not(mine))(far.start)
            pl.when(mine)(near.start)

    lane_of = lax.div(iota((8, SLOT), 1), CAP)
    large = jnp.full((8, SLOT), -1.0, F32)
    for c in range(4):
        for h in range(2):
            pltpu.make_async_copy(large_in.at[2 * c + h], large_in.at[2 * c + h], tr.at[2 * c + h]).wait()
        joined = jnp.maximum(large_in[2 * c], large_in[2 * c + 1])
        from_even = pltpu.roll(joined, lax.rem(CAP * (c - y) + SLOT, SLOT), 1)
        from_odd = pltpu.roll(joined, lax.rem(CAP * (c - z) + SLOT, SLOT), 1)
        large = jnp.where(lane_of == c, jnp.where(even, from_even, from_odd), large)
    for k in range(8):
        row = jnp.where(meta_recv[k, 0:1, :] < LARGE_IDS, large[k:k + 1], small_best[k:k + 1, :])
        final_send[k] = row

    def final_copy(k):
        return pltpu.make_async_remote_copy(
            final_send.at[k], final_recv.at[k], os.at[k], orr.at[k], (b, partner(k)), MESH)

    def final_start(k, carry):
        final_copy(k).start()
        return carry

    lax.fori_loop(1, 8, final_start, 0)
    final_recv[0] = final_send[0]

    def unpermute(k):
        out_ref[pl.ds(partner(k), 1), :] = jnp.sum(
            perms[k] * to_column(final_recv[k]), axis=0, keepdims=True)

    unpermute(0)

    def final_step(k, carry):
        final_copy(k).wait_recv()
        unpermute(k)
        return carry

    lax.fori_loop(1, 8, final_step, 0)

    def drain_line(k, carry):
        for copy in x_copies(k):
            copy.wait_send()
        final_copy(k).wait_send()
        return carry

    lax.fori_loop(1, 8, drain_line, 0)

    def drain_plane(k, carry):
        _, a, _ = axes(k)

        def piece(step, inner):
            for copy in first_copies(k, lax.rem(a + step, 4)):
                copy.wait_send()
            return inner

        lax.fori_loop(1, 4, piece, 0)
        split, stays = second_kind(k)

        @pl.when(split)
        def _():
            for n in range(2):
                for copy in split_copies(k, n):
                    copy.wait_send()

        @pl.when(jnp.logical_not(split | stays))
        def _():
            for copy in block_copies(k)[:2]:
                copy.wait_send()

        @pl.when(jnp.logical_not(busy))
        def _():
            for copy in turned_copies(k):
                copy.wait_send()

        return carry

    lax.fori_loop(0, 8, drain_plane, 0)

    @pl.when(busy)
    def _():
        def drain_share(k, carry):
            for copy in share_copies(k):
                copy.wait_send()
            return carry

        lax.fori_loop(0, 8, drain_share, 0)
        for i in range(16):
            pl.when(jnp.logical_not((b == i) & (host == core)))(result_copies(i)[0].wait_send)


def shards(embeddings, cluster_ids, orders):
    dma = pltpu.SemaphoreType.DMA
    vmem = pltpu.VMEM
    out = pl.pallas_call(
        kernel,
        out_shape=jax.ShapeDtypeStruct((8, SLOT), F32),
        in_specs=[pl.BlockSpec(memory_space=pl.ANY)] * 3,
        out_specs=pl.BlockSpec(memory_space=pltpu.VMEM),
        scratch_shapes=[
            vmem((8, SLOT, D), BF16),
            vmem((8, SLOT), jnp.int32),
            vmem((8, SLOT), jnp.int32),
            vmem((8, SLOT, D), BF16),
            vmem((8 * SLOT, D), BF16),
            vmem((8, 8, SLOT), F32),
            vmem((8, 8, SLOT), F32),
            vmem((8, SLOT, SLOT), F32),
            vmem((8, 1, SLOT), F32),
            vmem((8, 5 * CAP, D), BF16),
            vmem((8, 5, 1, SLOT), F32),
            vmem((8, 512, D), BF16),
            vmem((8, 16, 1, SLOT), F32),
            vmem((8, 8, SLOT), F32),
            vmem((4, 8, SLOT), F32),
            vmem((256, SLOT), F32),
            vmem((16, 8, SLOT), F32),
            vmem((8, 8, SLOT), F32),
            vmem((8, SLOT), F32),
            vmem((8, 1, SLOT), F32),
            vmem((8, 1, SLOT), F32),
            dma((8,)), dma((2,)),
            dma((8,)), dma((8,)), dma((8,)), dma((8,)),
            dma((8, 4)), dma((8, 2)), dma((8, 4)), dma((8, 2)),
            dma((8, 2)), dma((8,)), dma((8, 2)), dma((8,)),
            dma((8,)), dma((8,)), dma((8,)), dma((8,)),
            dma((16,)), dma((8,)),
            dma((8,)), dma((8,)),
        ],
        compiler_params=pltpu.CompilerParams(
            collective_id=0, has_side_effects=True, vmem_limit_bytes=60 * 1024 * 1024),
    )(embeddings.reshape(8, SLOT, D), cluster_ids.reshape(8, SLOT), orders.reshape(8, SLOT))
    return out.reshape(1, 1, 8, SLOT)


def solution(mesh):
    in_specs = (
        P("blk", "group", None, None, None),
        P("blk", "group", None, None),
        P("blk", "group", None, None),
    )
    out_specs = P("blk", "group", None, None)
    return jax.shard_map(shards, mesh=mesh, in_specs=in_specs, out_specs=out_specs, check_vma=False)
```

```python
import jax
import jax.numpy as jnp
from jax import lax
from jax.experimental import pallas as pl
from jax.experimental.pallas import tpu as pltpu
from jax.sharding import PartitionSpec as P

MESH = pl.DeviceIdType.MESH
F32 = jnp.float32
BF16 = jnp.bfloat16
D = 768
SLOT = 128
CAP = 32
LARGE_IDS = 32.0
NEVER = 1.0e9
EARLY = 5
LAG = 4
PASS = 2
ORDER = sum(way << (3 * step) for step, way in enumerate((0, 1, 2, 6, 3, 7, 4, 5)))


def flip(value, bits):
    out = 0
    for shift in (1, 2, 4):
        bit = lax.rem(lax.div(value, shift), 2) + lax.rem(lax.div(bits, shift), 2)
        out = out + shift * lax.rem(bit, 2)
    return out


def iota(shape, dim):
    return lax.broadcasted_iota(jnp.int32, shape, dim)


def to_column(row):
    eye = iota((SLOT, SLOT), 0) == iota((SLOT, SLOT), 1)
    return jnp.sum(jnp.where(eye, jnp.broadcast_to(row, (SLOT, SLOT)), 0.0), axis=1, keepdims=True)


def to_row(column):
    eye = iota((SLOT, SLOT), 0) == iota((SLOT, SLOT), 1)
    return jnp.sum(jnp.where(eye, jnp.broadcast_to(column, (SLOT, SLOT)), 0.0), axis=0, keepdims=True)


def product(query, keys):
    return lax.dot_general(query, keys, (((1,), (1,)), ((), ())), preferred_element_type=F32)


def permutation(ids, group):
    large = ids < LARGE_IDS
    label = jnp.where(large, ids - 4.0 * group.astype(F32), 4.0)
    sub = iota((SLOT, SLOT), 0)
    lane = iota((SLOT, SLOT), 1)
    before = jnp.where((to_column(label) == label) & (sub < lane), 1.0, 0.0)
    rank = jnp.sum(before, axis=0, keepdims=True)
    dest = jnp.where(large, CAP * label + rank, 4096.0)
    subf = sub.astype(F32)
    taken = jnp.where(dest == subf, 1024.0, 0.0) + jnp.where(dest < subf, 1.0, 0.0)
    slot = iota((SLOT, 1), 0).astype(F32)
    free = slot - jnp.sum(taken, axis=1, keepdims=True)
    return jnp.where((dest == subf) | (free == jnp.where(large, -8192.0, rank)), 1.0, 0.0)


def permuted_meta(ids, orders, perm):
    id_high = jnp.floor(ids * (1.0 / 32))
    order_high = jnp.floor(orders * (1.0 / 1024))
    rest = orders - 1024.0 * order_high
    order_mid = jnp.floor(rest * (1.0 / 32))
    at = iota((8, SLOT), 0)
    parts = jnp.zeros((8, SLOT), F32)
    pieces = (id_high, ids - 32.0 * id_high, order_high, order_mid, rest - 32.0 * order_mid)
    for index, piece in enumerate(pieces):
        parts = jnp.where(at == index, jnp.broadcast_to(piece, (8, SLOT)), parts)
    moved = product(parts, perm)
    slot_ids = moved[0:1] * 32.0 + moved[1:2]
    slot_orders = moved[2:3] * 1024.0 + moved[3:4] * 32.0 + moved[4:5]
    large_orders = jnp.where(slot_ids < LARGE_IDS, slot_orders, NEVER)
    out = jnp.where(at == 0, jnp.broadcast_to(slot_ids, (8, SLOT)), jnp.broadcast_to(slot_orders, (8, SLOT)))
    return jnp.where(at == 2, jnp.broadcast_to(large_orders, (8, SLOT)), out)


def kernel(
    emb, ids_in, orders_in, out_ref,
    raw, ids_ref, orders_ref, send, recv, meta_send, meta_recv, perms, plane_meta, mid, mid_meta,
    keys, key_meta, key_orders, best, found_ref, tile_send, large_in, small_best, final_send, final_recv,
    load_sem, info_sem, xs, xr, xms, xmr, ps, pr, pms, pmr, ss, sr, sms, smr, fs, fr, fms, fmr,
    ts, tr, os, orr, ready,
):
    b = lax.axis_index("blk")
    g = lax.axis_index("group")
    z, y = lax.div(b, 4), lax.rem(b, 4)
    x, core = lax.div(g, 2), lax.rem(g, 2)
    offset = lax.rem(y - z + 4, 4)
    busy = lax.rem(offset, 2) == 0
    host = lax.div(offset, 2)

    def relation(k):
        return lax.rem(lax.div(ORDER, lax.shift_left(1, 3 * k)), 8)

    def partner(k):
        return flip(g, relation(k))

    def load(k):
        return pltpu.make_async_copy(emb.at[partner(k)], raw.at[k], load_sem.at[k])

    info = (
        pltpu.make_async_copy(ids_in, ids_ref, info_sem.at[0]),
        pltpu.make_async_copy(orders_in, orders_ref, info_sem.at[1]),
    )
    for copy in info:
        copy.start()

    def load_step(k, carry):
        load(k).start()
        return carry

    lax.fori_loop(0, 8, load_step, 0)

    barrier = pltpu.get_barrier_semaphore()

    def greet(blk, group):
        pl.semaphore_signal(barrier, inc=1, device_id=(blk, group), device_id_type=MESH)

    for step in range(1, 4):
        for h in range(2):
            greet(4 * lax.rem(z + step, 4) + y, 2 * x + h)
            greet(4 * z + lax.rem(y + step, 4), 2 * x + h)
            greet(b, 2 * lax.rem(x + step, 4) + h)
    greet(b, 2 * x + 1 - core)

    def prepare(k):
        load(k).wait()
        owner = partner(k)
        ids = ids_ref[pl.ds(owner, 1), :].astype(F32)
        orders = orders_ref[pl.ds(owner, 1), :].astype(F32)
        perm = permutation(ids, owner)
        perms[k] = perm
        values = raw[k].astype(F32)
        total = jnp.sum(values * values, axis=1, keepdims=True)
        unit = (values * lax.rsqrt(total + 1e-06)).astype(BF16)
        rows = jnp.dot(perm.astype(BF16), unit, preferred_element_type=F32).astype(BF16)
        return rows, permuted_meta(ids, orders, perm)

    def block_of(k):
        return pl.ds(pl.multiple_of(k * SLOT, SLOT), SLOT)

    def x_copies(k):
        to = (b, partner(k))
        return (
            pltpu.make_async_remote_copy(send.at[k], recv.at[block_of(k)], xs.at[k], xr.at[k], to, MESH),
            pltpu.make_async_remote_copy(meta_send.at[k], meta_recv.at[k], xms.at[k], xmr.at[k], to, MESH),
        )

    def axes(k):
        staged = lax.rem(k, 2) == 0
        return staged, jnp.where(staged, z, y), jnp.where(staged, y, z)

    def device_at(staged, a, bb):
        return jnp.where(staged, 4 * a + bb, 4 * bb + a)

    def first_way(k, t):
        staged, a, bb = axes(k)
        end = lax.rem(t + 2 * core, 4)
        turned = (lax.rem(bb - end + 4, 4) == 2) & (lax.rem(a - t + 4, 2) == 1)
        return turned, device_at(staged, jnp.where(turned, a, t), jnp.where(turned, end, bb))

    def first_copies(k, t):
        staged, a, _ = axes(k)
        turned, stop = first_way(k, t)
        c = jnp.where(staged, t, lax.rem(t + 2 * core, 4))
        at = jnp.where(turned, 4, a)
        which = jnp.where(turned, 1, 0)
        rows = pl.ds(pl.multiple_of(k * SLOT + c * CAP, CAP), CAP)
        spot = pl.ds(pl.multiple_of(at * CAP, CAP), CAP)
        return (
            pltpu.make_async_remote_copy(
                recv.at[rows], mid.at[k, spot], ps.at[k, t], pr.at[k, which], (stop, g), MESH),
            pltpu.make_async_remote_copy(
                plane_meta.at[k], mid_meta.at[k, at], pms.at[k, t], pmr.at[k, which], (stop, g), MESH),
        )

    def first_near(k):
        staged, a, _ = axes(k)
        c = jnp.where(staged, a, lax.rem(a + 2 * core, 4))
        rows = pl.ds(pl.multiple_of(k * SLOT + c * CAP, CAP), CAP)
        spot = pl.ds(pl.multiple_of(a * CAP, CAP), CAP)
        return (
            pltpu.make_async_copy(recv.at[rows], mid.at[k, spot], pr.at[k, 0]),
            pltpu.make_async_copy(plane_meta.at[k], mid_meta.at[k, a], pmr.at[k, 0]),
        )

    def direct_copies(k, t):
        c = lax.rem(t + 2 * core, 4)
        to = (4 * c + t, 2 * x + lax.div(z, 2))
        rows = recv.at[pl.ds(pl.multiple_of(k * SLOT + c * CAP, CAP), CAP)]
        spot = keys.at[k, pl.ds(pl.multiple_of(b * CAP, CAP), CAP)]
        meta, meta_spot = plane_meta.at[k], key_meta.at[k, b]
        return (
            pltpu.make_async_remote_copy(rows, spot, ps.at[k, t], sr.at[k], to, MESH),
            pltpu.make_async_remote_copy(meta, meta_spot, pms.at[k, t], smr.at[k], to, MESH),
            pltpu.make_async_copy(rows, spot, sr.at[k]),
            pltpu.make_async_copy(meta, meta_spot, smr.at[k]),
        )

    def direct_near(t):
        return (4 * lax.rem(t + 2 * core, 4) + t == b) & (lax.div(z, 2) == core)

    def send_first(k):
        plane_meta[k] = meta_recv[k, 2:3, :]
        staged, a, _ = axes(k)

        def piece(step, carry):
            t = lax.rem(a + step, 4)
            turned, _ = first_way(k, t)

            @pl.when(staged | turned)
            def _():
                rows, meta = first_copies(k, t)
                meta.start()
                rows.start()

            @pl.when(jnp.logical_not(staged | turned | direct_near(t)))
            def _():
                rows, meta, _, _ = direct_copies(k, t)
                meta.start()
                rows.start()

            return carry

        lax.fori_loop(1, 4, piece, 0)

        @pl.when(staged)
        def _():
            for copy in first_near(k):
                copy.start()

        @pl.when(jnp.logical_not(staged))
        def _():
            far_rows, far_meta, near_rows, near_meta = direct_copies(k, a)

            @pl.when(direct_near(a))
            def _():
                near_meta.start()
                near_rows.start()

            @pl.when(jnp.logical_not(direct_near(a)))
            def _():
                far_meta.start()
                far_rows.start()

    def piece_copies(k, source, place, blk, sem):
        to = (blk, 2 * x + lax.div(place, 8))
        rows = pl.ds(pl.multiple_of(source * CAP, CAP), CAP)
        spot = pl.ds(pl.multiple_of(place * CAP, CAP), CAP)
        return (
            pltpu.make_async_remote_copy(
                mid.at[k, rows], keys.at[k, spot], ss.at[k, sem], sr.at[k], to, MESH),
            pltpu.make_async_remote_copy(
                mid_meta.at[k, source], key_meta.at[k, place], sms.at[k, sem], smr.at[k], to, MESH),
        )

    def block_copies(k):
        staged, a, bb = axes(k)
        blk = device_at(staged, a, lax.rem(a + 2 * core, 4))
        to = (blk, 2 * x + lax.div(bb, 2))
        rows = mid.at[k, pl.ds(0, SLOT)]
        spot = keys.at[k, pl.ds(pl.multiple_of(bb * SLOT, SLOT), SLOT)]
        meta = mid_meta.at[k, pl.ds(0, 4)]
        meta_spot = key_meta.at[k, pl.ds(pl.multiple_of(bb * 4, 4), 4)]
        return (
            pltpu.make_async_remote_copy(rows, spot, ss.at[k, 0], sr.at[k], to, MESH),
            pltpu.make_async_remote_copy(meta, meta_spot, sms.at[k, 0], smr.at[k], to, MESH),
            pltpu.make_async_copy(rows, spot, sr.at[k]),
            pltpu.make_async_copy(meta, meta_spot, smr.at[k]),
        )

    def second_kind(k):
        _, a, bb = axes(k)
        split = lax.rem(bb - a - 2 * core + 8, 4) == 2
        stays = busy & (host == core) & (lax.div(bb, 2) == core)
        return split, stays

    def split_copies(k, n):
        staged, a, bb = axes(k)
        source = lax.rem(a + 2 * n, 4)
        return piece_copies(k, source, 4 * bb + source, device_at(staged, a, lax.rem(a + 2 * core, 4)), n)

    def turned_copies(k):
        staged, a, bb = axes(k)
        blk = device_at(staged, lax.rem(bb + 2 * core, 4), bb)
        return piece_copies(k, 4, 4 * lax.rem(bb + 2, 4) + a, blk, 1)

    def send_second(k):
        staged, _, _ = axes(k)
        split, stays = second_kind(k)

        @pl.when(staged & split)
        def _():
            half_meta = mid_meta.at[k, pl.ds(0, 2)]
            half_rows = mid.at[k, pl.ds(0, 2 * CAP)]
            pltpu.make_async_copy(half_meta, half_meta, pmr.at[k, 0]).wait()
            pltpu.make_async_copy(half_rows, half_rows, pr.at[k, 0]).wait()
            for n in range(2):
                rows, meta = split_copies(k, n)
                meta.start()
                rows.start()

        @pl.when(staged & jnp.logical_not(split))
        def _():
            all_meta = mid_meta.at[k, pl.ds(0, 4)]
            all_rows = mid.at[k, pl.ds(0, SLOT)]
            pltpu.make_async_copy(all_meta, all_meta, pmr.at[k, 0]).wait()
            pltpu.make_async_copy(all_rows, all_rows, pr.at[k, 0]).wait()
            far_rows, far_meta, near_rows, near_meta = block_copies(k)

            @pl.when(jnp.logical_not(stays))
            def _():
                far_meta.start()
                far_rows.start()

            @pl.when(stays)
            def _():
                near_meta.start()
                near_rows.start()

        @pl.when(jnp.logical_not(busy))
        def _():
            rows, meta = turned_copies(k)
            one_meta = mid_meta.at[k, 4]
            one_rows = mid.at[k, pl.ds(4 * CAP, CAP)]
            pltpu.make_async_copy(one_meta, one_meta, pmr.at[k, 1]).wait()
            pltpu.make_async_copy(one_rows, one_rows, pr.at[k, 1]).wait()
            meta.start()
            rows.start()

    def share_copies(k):
        to = (b, 2 * x + 1 - core)
        rows = pl.ds(pl.multiple_of(core * 256, 256), 256)
        sources = pl.ds(pl.multiple_of(core * 8, 8), 8)
        return (
            pltpu.make_async_remote_copy(keys.at[k, rows], keys.at[k, rows], fs.at[k], fr.at[k], to, MESH),
            pltpu.make_async_remote_copy(
                key_meta.at[k, sources], key_meta.at[k, sources], fms.at[k], fmr.at[k], to, MESH),
        )

    def share(k):
        rows = keys.at[k, pl.ds(pl.multiple_of(core * 256, 256), 256)]
        sources = key_meta.at[k, pl.ds(pl.multiple_of(core * 8, 8), 8)]
        pltpu.make_async_copy(sources, sources, smr.at[k]).wait()
        pltpu.make_async_copy(rows, rows, sr.at[k]).wait()
        for copy in share_copies(k):
            copy.start()

    lane_part = lax.div(iota((1, SLOT), 1), CAP)

    def merge_orders(k, u):
        merged = jnp.zeros((1, SLOT), F32)
        for j in range(4):
            shift = lax.rem(CAP * (j - z) + SLOT, SLOT)
            merged = jnp.where(lane_part == j, pltpu.roll(key_meta[k, 4 * u + j], shift, 1), merged)
        key_orders[k, pl.ds(u, 1), :] = merged

    def query_of(k):
        places = [to_column(key_orders[k, pl.ds(2 * core + i, 1), :]) for i in range(2)]
        return keys[k, pl.ds(pl.multiple_of(core * 256, 256), 256)], jnp.concatenate(places, axis=0)

    def against(query, places, j, found, one_way):
        for h in range(2):
            scores = product(query, keys[j, h * 256:(h + 1) * 256])
            for i in range(2):
                u = 2 * h + i
                part = scores[:, i * SLOT:(i + 1) * SLOT]
                earlier = key_orders[j, u:u + 1, :] < places
                found = jnp.maximum(found, jnp.where(earlier, part, -1.0))
                if not one_way:
                    other = jnp.max(jnp.where(earlier, -1.0, part), axis=0, keepdims=True)
                    best[u, pl.ds(j, 1), :] = jnp.maximum(best[u, pl.ds(j, 1), :], other)
        return found

    def compare_old(k):
        for i in range(2):
            merge_orders(k, 2 * core + i)
        query, places = query_of(k)
        start = jnp.full((256, SLOT), -1.0, F32)
        if isinstance(k, int):
            found = start
            for j in range(k):
                found = against(query, places, j, found, False)
            found_ref[...] = found
            return

        def two(j, found):
            return against(query, places, 2 * j + 1, against(query, places, 2 * j, found, False), False)

        found_ref[...] = lax.fori_loop(0, lax.div(k, 2), two, start)

        @pl.when(lax.rem(k, 2) == 1)
        def _():
            found_ref[...] = against(query, places, k - 1, found_ref[...], False)

    def compare_same(k):
        for copy in share_copies(k):
            copy.wait_recv()
        for i in range(2):
            merge_orders(k, 2 * (1 - core) + i)
        query, places = query_of(k)
        found = against(query, places, k, found_ref[...], True)
        column = jnp.max(found, axis=1, keepdims=True)
        for i in range(2):
            best[2 * core + i, pl.ds(k, 1), :] = to_row(column[i * SLOT:(i + 1) * SLOT])

    def take(k):
        share(k)
        if not isinstance(k, int):
            pl.when(k >= 1)(lambda: compare_same(k - 1))
        elif k >= 1:
            compare_same(k - 1)
        compare_old(k)

    best[...] = jnp.full(best.shape, -1.0, F32)
    for copy in info:
        copy.wait()

    rows, meta = prepare(0)
    recv[0:SLOT] = rows
    meta_recv[0] = meta

    def prepare_step(k, carry):
        rows, meta = prepare(k)
        send[k] = rows
        meta_send[k] = meta
        return carry

    def leave_step(k, carry):
        for copy in x_copies(k):
            copy.start()
        return carry

    lax.fori_loop(1, EARLY, prepare_step, 0)
    pl.semaphore_wait(barrier, 19)
    for step in range(1, 4):
        pl.semaphore_signal(ready, inc=1, device_id=(4 * lax.rem(z + step, 4) + y, g), device_id_type=MESH)
    lax.fori_loop(1, EARLY, leave_step, 0)
    send_first(0)
    lax.fori_loop(EARLY, 8, lambda k, carry: leave_step(k, prepare_step(k, carry)), 0)
    pl.semaphore_wait(ready, 3)

    def pass_on(k, carry):
        for copy in x_copies(k):
            copy.wait_recv()
        send_first(k)
        pl.when(k >= PASS)(lambda: send_second(k - PASS))

        @pl.when(busy & (k >= LAG))
        def _():
            take(k - LAG)

        return carry

    lax.fori_loop(1, 8, pass_on, 0)
    lax.fori_loop(8 - PASS, 8, lambda k, carry: (send_second(k), carry)[1], 0)

    def small(q, carry):
        query = recv[pl.ds(pl.multiple_of(q * 256, 256), 256)]
        labels = jnp.concatenate([to_column(meta_recv[2 * q + i, 0:1, :]) for i in range(2)], axis=0)
        labels = jnp.where(labels < LARGE_IDS, -1.0, labels)
        places = jnp.concatenate([to_column(meta_recv[2 * q + i, 1:2, :]) for i in range(2)], axis=0)
        found = jnp.full((256, SLOT), -1.0, F32)
        for j in range(4):
            scores = product(query, recv[j * 256:(j + 1) * 256])
            for i in range(2):
                match = (meta_recv[2 * j + i, 0:1, :] == labels) & (meta_recv[2 * j + i, 1:2, :] < places)
                found = jnp.maximum(found, jnp.where(match, scores[:, i * SLOT:(i + 1) * SLOT], -1.0))
        column = jnp.max(found, axis=1, keepdims=True)
        for i in range(2):
            small_best[pl.ds(2 * q + i, 1), :] = to_row(column[i * SLOT:(i + 1) * SLOT])
        return carry

    lax.fori_loop(0, 4, small, 0)

    def result_copies(i):
        spot = 2 * z + core
        return (
            pltpu.make_async_remote_copy(
                tile_send.at[i], large_in.at[spot], ts.at[i], tr.at[spot], (i, 2 * x + host), MESH),
            pltpu.make_async_copy(tile_send.at[i], large_in.at[spot], tr.at[spot]),
        )

    even = lax.rem(iota((8, SLOT), 0), 2) == 0

    @pl.when(busy)
    def _():
        if LAG > 2:
            lax.fori_loop(8 - LAG, 6, lambda k, carry: (take(k), carry)[1], 0)
        take(6)
        take(7)
        compare_same(7)
        for i in range(16):
            tile_send[i] = jnp.where(even, best[i % 4], best[i // 4])
            far, near = result_copies(i)
            mine = (b == i) & (host == core)
            pl.when(jnp.logical_not(mine))(far.start)
            pl.when(mine)(near.start)

    def drain_line(k, carry):
        for copy in x_copies(k):
            copy.wait_send()
        return carry

    lax.fori_loop(1, 8, drain_line, 0)

    def drain_plane(k, carry):
        staged, a, _ = axes(k)

        def piece(step, inner):
            t = lax.rem(a + step, 4)
            for copy in first_copies(k, t):
                copy.wait_send()
            return inner

        lax.fori_loop(1, 4, piece, 0)

        @pl.when(jnp.logical_not(staged | direct_near(a)))
        def _():
            for copy in direct_copies(k, a)[:2]:
                copy.wait_send()

        split, stays = second_kind(k)

        @pl.when(staged & split)
        def _():
            for n in range(2):
                for copy in split_copies(k, n):
                    copy.wait_send()

        @pl.when(staged & jnp.logical_not(split | stays))
        def _():
            for copy in block_copies(k)[:2]:
                copy.wait_send()

        @pl.when(jnp.logical_not(busy))
        def _():
            for copy in turned_copies(k):
                copy.wait_send()

        return carry

    lax.fori_loop(0, 8, drain_plane, 0)

    @pl.when(busy)
    def _():
        def drain_share(k, carry):
            for copy in share_copies(k):
                copy.wait_send()
            return carry

        lax.fori_loop(0, 8, drain_share, 0)
        for i in range(16):
            pl.when(jnp.logical_not((b == i) & (host == core)))(result_copies(i)[0].wait_send)

    lane_of = lax.div(iota((8, SLOT), 1), CAP)
    large = jnp.full((8, SLOT), -1.0, F32)
    for c in range(4):
        for h in range(2):
            pltpu.make_async_copy(large_in.at[2 * c + h], large_in.at[2 * c + h], tr.at[2 * c + h]).wait()
        joined = jnp.maximum(large_in[2 * c], large_in[2 * c + 1])
        from_even = pltpu.roll(joined, lax.rem(CAP * (c - z) + SLOT, SLOT), 1)
        from_odd = pltpu.roll(joined, lax.rem(CAP * (c - y) + SLOT, SLOT), 1)
        large = jnp.where(lane_of == c, jnp.where(even, from_even, from_odd), large)
    for k in range(8):
        row = jnp.where(meta_recv[k, 0:1, :] < LARGE_IDS, large[k:k + 1], small_best[k:k + 1, :])
        final_send[k] = row

    def final_copy(k):
        return pltpu.make_async_remote_copy(
            final_send.at[k], final_recv.at[k], os.at[k], orr.at[k], (b, partner(k)), MESH)

    def final_start(k, carry):
        final_copy(k).start()
        return carry

    lax.fori_loop(1, 8, final_start, 0)
    final_recv[0] = final_send[0]

    def unpermute(k):
        out_ref[pl.ds(partner(k), 1), :] = jnp.sum(
            perms[k] * to_column(final_recv[k]), axis=0, keepdims=True)

    unpermute(0)

    def final_step(k, carry):
        final_copy(k).wait_recv()
        unpermute(k)
        return carry

    lax.fori_loop(1, 8, final_step, 0)

    lax.fori_loop(1, 8, lambda k, carry: (final_copy(k).wait_send(), carry)[1], 0)


def shards(embeddings, cluster_ids, orders):
    dma = pltpu.SemaphoreType.DMA
    vmem = pltpu.VMEM
    out = pl.pallas_call(
        kernel,
        out_shape=jax.ShapeDtypeStruct((8, SLOT), F32),
        in_specs=[pl.BlockSpec(memory_space=pl.ANY)] * 3,
        out_specs=pl.BlockSpec(memory_space=pltpu.VMEM),
        scratch_shapes=[
            vmem((8, SLOT, D), BF16),
            vmem((8, SLOT), jnp.int32),
            vmem((8, SLOT), jnp.int32),
            vmem((8, SLOT, D), BF16),
            vmem((8 * SLOT, D), BF16),
            vmem((8, 8, SLOT), F32),
            vmem((8, 8, SLOT), F32),
            vmem((8, SLOT, SLOT), F32),
            vmem((8, 1, SLOT), F32),
            vmem((8, 5 * CAP, D), BF16),
            vmem((8, 5, 1, SLOT), F32),
            vmem((8, 512, D), BF16),
            vmem((8, 16, 1, SLOT), F32),
            vmem((8, 8, SLOT), F32),
            vmem((4, 8, SLOT), F32),
            vmem((256, SLOT), F32),
            vmem((16, 8, SLOT), F32),
            vmem((8, 8, SLOT), F32),
            vmem((8, SLOT), F32),
            vmem((8, 1, SLOT), F32),
            vmem((8, 1, SLOT), F32),
            dma((8,)), dma((2,)),
            dma((8,)), dma((8,)), dma((8,)), dma((8,)),
            dma((8, 4)), dma((8, 2)), dma((8, 4)), dma((8, 2)),
            dma((8, 2)), dma((8,)), dma((8, 2)), dma((8,)),
            dma((8,)), dma((8,)), dma((8,)), dma((8,)),
            dma((16,)), dma((8,)),
            dma((8,)), dma((8,)),
            pltpu.SemaphoreType.REGULAR,
        ],
        compiler_params=pltpu.CompilerParams(
            collective_id=0, has_side_effects=True, vmem_limit_bytes=60 * 1024 * 1024),
    )(embeddings.reshape(8, SLOT, D), cluster_ids.reshape(8, SLOT), orders.reshape(8, SLOT))
    return out.reshape(1, 1, 8, SLOT)


def solution(mesh):
    in_specs = (
        P("blk", "group", None, None, None),
        P("blk", "group", None, None),
        P("blk", "group", None, None),
    )
    out_specs = P("blk", "group", None, None)
    return jax.shard_map(shards, mesh=mesh, in_specs=in_specs, out_specs=out_specs, check_vma=False)
```

```python
import jax
import jax.numpy as jnp
from jax import lax
from jax.experimental import pallas as pl
from jax.experimental.pallas import tpu as pltpu
from jax.sharding import PartitionSpec as P

MESH = pl.DeviceIdType.MESH
F32 = jnp.float32
BF16 = jnp.bfloat16
D = 768
SLOT = 128
CAP = 32
LARGE_IDS = 32.0
NEVER = 1.0e9
EARLY = 4
LAG = 4
PASS = 2
ORDER = sum(way << (3 * step) for step, way in enumerate((0, 1, 2, 6, 3, 7, 4, 5)))


def flip(value, bits):
    out = 0
    for shift in (1, 2, 4):
        bit = lax.rem(lax.div(value, shift), 2) + lax.rem(lax.div(bits, shift), 2)
        out = out + shift * lax.rem(bit, 2)
    return out


def iota(shape, dim):
    return lax.broadcasted_iota(jnp.int32, shape, dim)


def to_column(row):
    eye = iota((SLOT, SLOT), 0) == iota((SLOT, SLOT), 1)
    return jnp.sum(jnp.where(eye, jnp.broadcast_to(row, (SLOT, SLOT)), 0.0), axis=1, keepdims=True)


def to_row(column):
    eye = iota((SLOT, SLOT), 0) == iota((SLOT, SLOT), 1)
    return jnp.sum(jnp.where(eye, jnp.broadcast_to(column, (SLOT, SLOT)), 0.0), axis=0, keepdims=True)


def product(query, keys):
    return lax.dot_general(query, keys, (((1,), (1,)), ((), ())), preferred_element_type=F32)


def permutation(ids, group):
    large = ids < LARGE_IDS
    label = jnp.where(large, ids - 4.0 * group.astype(F32), 4.0)
    sub = iota((SLOT, SLOT), 0)
    lane = iota((SLOT, SLOT), 1)
    before = jnp.where((to_column(label) == label) & (sub < lane), 1.0, 0.0)
    rank = jnp.sum(before, axis=0, keepdims=True)
    dest = jnp.where(large, CAP * label + rank, 4096.0)
    subf = sub.astype(F32)
    taken = jnp.where(dest == subf, 1024.0, 0.0) + jnp.where(dest < subf, 1.0, 0.0)
    slot = iota((SLOT, 1), 0).astype(F32)
    free = slot - jnp.sum(taken, axis=1, keepdims=True)
    return jnp.where((dest == subf) | (free == jnp.where(large, -8192.0, rank)), 1.0, 0.0)


def permuted_meta(ids, orders, perm):
    id_high = jnp.floor(ids * (1.0 / 32))
    order_high = jnp.floor(orders * (1.0 / 1024))
    rest = orders - 1024.0 * order_high
    order_mid = jnp.floor(rest * (1.0 / 32))
    at = iota((8, SLOT), 0)
    parts = jnp.zeros((8, SLOT), F32)
    pieces = (id_high, ids - 32.0 * id_high, order_high, order_mid, rest - 32.0 * order_mid)
    for index, piece in enumerate(pieces):
        parts = jnp.where(at == index, jnp.broadcast_to(piece, (8, SLOT)), parts)
    moved = product(parts, perm)
    slot_ids = moved[0:1] * 32.0 + moved[1:2]
    slot_orders = moved[2:3] * 1024.0 + moved[3:4] * 32.0 + moved[4:5]
    large_orders = jnp.where(slot_ids < LARGE_IDS, slot_orders, NEVER)
    out = jnp.where(at == 0, jnp.broadcast_to(slot_ids, (8, SLOT)), jnp.broadcast_to(slot_orders, (8, SLOT)))
    return jnp.where(at == 2, jnp.broadcast_to(large_orders, (8, SLOT)), out)


def kernel(
    emb, ids_in, orders_in, out_ref,
    raw, ids_ref, orders_ref, send, recv, meta_send, meta_recv, perms, plane_meta, mid, mid_meta,
    keys, key_meta, key_orders, best, found_ref, tile_send, large_in, small_best, final_send, final_recv,
    load_sem, info_sem, xs, xr, xms, xmr, ps, pr, pms, pmr, ss, sr, sms, smr, fs, fr, fms, fmr,
    ts, tr, os, orr, ready,
):
    b = lax.axis_index("blk")
    g = lax.axis_index("group")
    z, y = lax.div(b, 4), lax.rem(b, 4)
    x, core = lax.div(g, 2), lax.rem(g, 2)
    offset = lax.rem(y - z + 4, 4)
    busy = lax.rem(offset, 2) == 0
    host = lax.div(offset, 2)

    def relation(k):
        return lax.rem(lax.div(ORDER, lax.shift_left(1, 3 * k)), 8)

    def partner(k):
        return flip(g, relation(k))

    def load(k):
        return pltpu.make_async_copy(emb.at[partner(k)], raw.at[k], load_sem.at[k])

    info = (
        pltpu.make_async_copy(ids_in, ids_ref, info_sem.at[0]),
        pltpu.make_async_copy(orders_in, orders_ref, info_sem.at[1]),
    )
    for copy in info:
        copy.start()

    def load_step(k, carry):
        load(k).start()
        return carry

    lax.fori_loop(0, 8, load_step, 0)

    barrier = pltpu.get_barrier_semaphore()

    def greet(blk, group):
        pl.semaphore_signal(barrier, inc=1, device_id=(blk, group), device_id_type=MESH)

    for step in range(1, 4):
        for h in range(2):
            greet(4 * lax.rem(z + step, 4) + y, 2 * x + h)
            greet(4 * z + lax.rem(y + step, 4), 2 * x + h)
            greet(b, 2 * lax.rem(x + step, 4) + h)
    greet(b, 2 * x + 1 - core)

    def prepare(k):
        load(k).wait()
        owner = partner(k)
        ids = ids_ref[pl.ds(owner, 1), :].astype(F32)
        orders = orders_ref[pl.ds(owner, 1), :].astype(F32)
        perm = permutation(ids, owner)
        perms[k] = perm
        values = raw[k].astype(F32)
        total = jnp.sum(values * values, axis=1, keepdims=True)
        unit = (values * lax.rsqrt(total + 1e-06)).astype(BF16)
        rows = jnp.dot(perm.astype(BF16), unit, preferred_element_type=F32).astype(BF16)
        return rows, permuted_meta(ids, orders, perm)

    def block_of(k):
        return pl.ds(pl.multiple_of(k * SLOT, SLOT), SLOT)

    def x_copies(k):
        to = (b, partner(k))
        return (
            pltpu.make_async_remote_copy(send.at[k], recv.at[block_of(k)], xs.at[k], xr.at[k], to, MESH),
            pltpu.make_async_remote_copy(meta_send.at[k], meta_recv.at[k], xms.at[k], xmr.at[k], to, MESH),
        )

    def axes(k):
        staged = lax.rem(k, 2) == 0
        return staged, jnp.where(staged, z, y), jnp.where(staged, y, z)

    def device_at(staged, a, bb):
        return jnp.where(staged, 4 * a + bb, 4 * bb + a)

    def first_way(k, t):
        staged, a, bb = axes(k)
        end = lax.rem(t + 2 * core, 4)
        turned = (lax.rem(bb - end + 4, 4) == 2) & (lax.rem(a - t + 4, 2) == 1)
        return turned, device_at(staged, jnp.where(turned, a, t), jnp.where(turned, end, bb))

    def first_copies(k, t):
        staged, a, _ = axes(k)
        turned, stop = first_way(k, t)
        c = jnp.where(staged, t, lax.rem(t + 2 * core, 4))
        at = jnp.where(turned, 4, a)
        which = jnp.where(turned, 1, 0)
        rows = pl.ds(pl.multiple_of(k * SLOT + c * CAP, CAP), CAP)
        spot = pl.ds(pl.multiple_of(at * CAP, CAP), CAP)
        return (
            pltpu.make_async_remote_copy(
                recv.at[rows], mid.at[k, spot], ps.at[k, t], pr.at[k, which], (stop, g), MESH),
            pltpu.make_async_remote_copy(
                plane_meta.at[k], mid_meta.at[k, at], pms.at[k, t], pmr.at[k, which], (stop, g), MESH),
        )

    def first_near(k):
        staged, a, _ = axes(k)
        c = jnp.where(staged, a, lax.rem(a + 2 * core, 4))
        rows = pl.ds(pl.multiple_of(k * SLOT + c * CAP, CAP), CAP)
        spot = pl.ds(pl.multiple_of(a * CAP, CAP), CAP)
        return (
            pltpu.make_async_copy(recv.at[rows], mid.at[k, spot], pr.at[k, 0]),
            pltpu.make_async_copy(plane_meta.at[k], mid_meta.at[k, a], pmr.at[k, 0]),
        )

    def direct_copies(k, t):
        c = lax.rem(t + 2 * core, 4)
        to = (4 * c + t, 2 * x + lax.div(z, 2))
        rows = recv.at[pl.ds(pl.multiple_of(k * SLOT + c * CAP, CAP), CAP)]
        spot = keys.at[k, pl.ds(pl.multiple_of(b * CAP, CAP), CAP)]
        meta, meta_spot = plane_meta.at[k], key_meta.at[k, b]
        return (
            pltpu.make_async_remote_copy(rows, spot, ps.at[k, t], sr.at[k], to, MESH),
            pltpu.make_async_remote_copy(meta, meta_spot, pms.at[k, t], smr.at[k], to, MESH),
            pltpu.make_async_copy(rows, spot, sr.at[k]),
            pltpu.make_async_copy(meta, meta_spot, smr.at[k]),
        )

    def direct_near(t):
        return (4 * lax.rem(t + 2 * core, 4) + t == b) & (lax.div(z, 2) == core)

    def send_first(k):
        plane_meta[k] = meta_recv[k, 2:3, :]
        staged, a, _ = axes(k)

        def piece(step, carry):
            t = lax.rem(a + step, 4)
            turned, _ = first_way(k, t)

            @pl.when(staged | turned)
            def _():
                rows, meta = first_copies(k, t)
                meta.start()
                rows.start()

            @pl.when(jnp.logical_not(staged | turned | direct_near(t)))
            def _():
                rows, meta, _, _ = direct_copies(k, t)
                meta.start()
                rows.start()

            return carry

        lax.fori_loop(1, 4, piece, 0)

        @pl.when(staged)
        def _():
            for copy in first_near(k):
                copy.start()

        @pl.when(jnp.logical_not(staged))
        def _():
            far_rows, far_meta, near_rows, near_meta = direct_copies(k, a)

            @pl.when(direct_near(a))
            def _():
                near_meta.start()
                near_rows.start()

            @pl.when(jnp.logical_not(direct_near(a)))
            def _():
                far_meta.start()
                far_rows.start()

    def piece_copies(k, source, place, blk, sem):
        to = (blk, 2 * x + lax.div(place, 8))
        rows = pl.ds(pl.multiple_of(source * CAP, CAP), CAP)
        spot = pl.ds(pl.multiple_of(place * CAP, CAP), CAP)
        return (
            pltpu.make_async_remote_copy(
                mid.at[k, rows], keys.at[k, spot], ss.at[k, sem], sr.at[k], to, MESH),
            pltpu.make_async_remote_copy(
                mid_meta.at[k, source], key_meta.at[k, place], sms.at[k, sem], smr.at[k], to, MESH),
        )

    def block_copies(k):
        staged, a, bb = axes(k)
        blk = device_at(staged, a, lax.rem(a + 2 * core, 4))
        to = (blk, 2 * x + lax.div(bb, 2))
        rows = mid.at[k, pl.ds(0, SLOT)]
        spot = keys.at[k, pl.ds(pl.multiple_of(bb * SLOT, SLOT), SLOT)]
        meta = mid_meta.at[k, pl.ds(0, 4)]
        meta_spot = key_meta.at[k, pl.ds(pl.multiple_of(bb * 4, 4), 4)]
        return (
            pltpu.make_async_remote_copy(rows, spot, ss.at[k, 0], sr.at[k], to, MESH),
            pltpu.make_async_remote_copy(meta, meta_spot, sms.at[k, 0], smr.at[k], to, MESH),
            pltpu.make_async_copy(rows, spot, sr.at[k]),
            pltpu.make_async_copy(meta, meta_spot, smr.at[k]),
        )

    def second_kind(k):
        _, a, bb = axes(k)
        split = lax.rem(bb - a - 2 * core + 8, 4) == 2
        stays = busy & (host == core) & (lax.div(bb, 2) == core)
        return split, stays

    def split_copies(k, n):
        staged, a, bb = axes(k)
        source = lax.rem(a + 2 * n, 4)
        return piece_copies(k, source, 4 * bb + source, device_at(staged, a, lax.rem(a + 2 * core, 4)), n)

    def turned_copies(k):
        staged, a, bb = axes(k)
        blk = device_at(staged, lax.rem(bb + 2 * core, 4), bb)
        return piece_copies(k, 4, 4 * lax.rem(bb + 2, 4) + a, blk, 1)

    def send_second(k):
        staged, _, _ = axes(k)
        split, stays = second_kind(k)

        @pl.when(staged & split)
        def _():
            half_meta = mid_meta.at[k, pl.ds(0, 2)]
            half_rows = mid.at[k, pl.ds(0, 2 * CAP)]
            pltpu.make_async_copy(half_meta, half_meta, pmr.at[k, 0]).wait()
            pltpu.make_async_copy(half_rows, half_rows, pr.at[k, 0]).wait()
            for n in range(2):
                rows, meta = split_copies(k, n)
                meta.start()
                rows.start()

        @pl.when(staged & jnp.logical_not(split))
        def _():
            all_meta = mid_meta.at[k, pl.ds(0, 4)]
            all_rows = mid.at[k, pl.ds(0, SLOT)]
            pltpu.make_async_copy(all_meta, all_meta, pmr.at[k, 0]).wait()
            pltpu.make_async_copy(all_rows, all_rows, pr.at[k, 0]).wait()
            far_rows, far_meta, near_rows, near_meta = block_copies(k)

            @pl.when(jnp.logical_not(stays))
            def _():
                far_meta.start()
                far_rows.start()

            @pl.when(stays)
            def _():
                near_meta.start()
                near_rows.start()

        @pl.when(jnp.logical_not(busy))
        def _():
            rows, meta = turned_copies(k)
            one_meta = mid_meta.at[k, 4]
            one_rows = mid.at[k, pl.ds(4 * CAP, CAP)]
            pltpu.make_async_copy(one_meta, one_meta, pmr.at[k, 1]).wait()
            pltpu.make_async_copy(one_rows, one_rows, pr.at[k, 1]).wait()
            meta.start()
            rows.start()

    def share_copies(k):
        to = (b, 2 * x + 1 - core)
        rows = pl.ds(pl.multiple_of(core * 256, 256), 256)
        sources = pl.ds(pl.multiple_of(core * 8, 8), 8)
        return (
            pltpu.make_async_remote_copy(keys.at[k, rows], keys.at[k, rows], fs.at[k], fr.at[k], to, MESH),
            pltpu.make_async_remote_copy(
                key_meta.at[k, sources], key_meta.at[k, sources], fms.at[k], fmr.at[k], to, MESH),
        )

    def share(k):
        rows = keys.at[k, pl.ds(pl.multiple_of(core * 256, 256), 256)]
        sources = key_meta.at[k, pl.ds(pl.multiple_of(core * 8, 8), 8)]
        pltpu.make_async_copy(sources, sources, smr.at[k]).wait()
        pltpu.make_async_copy(rows, rows, sr.at[k]).wait()
        for copy in share_copies(k):
            copy.start()

    lane_part = lax.div(iota((1, SLOT), 1), CAP)

    def merge_orders(k, u):
        merged = jnp.zeros((1, SLOT), F32)
        for j in range(4):
            shift = lax.rem(CAP * (j - z) + SLOT, SLOT)
            merged = jnp.where(lane_part == j, pltpu.roll(key_meta[k, 4 * u + j], shift, 1), merged)
        key_orders[k, pl.ds(u, 1), :] = merged

    def query_of(k):
        places = [to_column(key_orders[k, pl.ds(2 * core + i, 1), :]) for i in range(2)]
        return keys[k, pl.ds(pl.multiple_of(core * 256, 256), 256)], jnp.concatenate(places, axis=0)

    def against(query, places, j, found, one_way):
        for h in range(2):
            scores = product(query, keys[j, h * 256:(h + 1) * 256])
            for i in range(2):
                u = 2 * h + i
                part = scores[:, i * SLOT:(i + 1) * SLOT]
                earlier = key_orders[j, u:u + 1, :] < places
                found = jnp.maximum(found, jnp.where(earlier, part, -1.0))
                if not one_way:
                    other = jnp.max(jnp.where(earlier, -1.0, part), axis=0, keepdims=True)
                    best[u, pl.ds(j, 1), :] = jnp.maximum(best[u, pl.ds(j, 1), :], other)
        return found

    def compare_old(k):
        for i in range(2):
            merge_orders(k, 2 * core + i)
        query, places = query_of(k)
        start = jnp.full((256, SLOT), -1.0, F32)
        if isinstance(k, int):
            found = start
            for j in range(k):
                found = against(query, places, j, found, False)
            found_ref[...] = found
            return

        def two(j, found):
            return against(query, places, 2 * j + 1, against(query, places, 2 * j, found, False), False)

        found_ref[...] = lax.fori_loop(0, lax.div(k, 2), two, start)

        @pl.when(lax.rem(k, 2) == 1)
        def _():
            found_ref[...] = against(query, places, k - 1, found_ref[...], False)

    def compare_same(k):
        for copy in share_copies(k):
            copy.wait_recv()
        for i in range(2):
            merge_orders(k, 2 * (1 - core) + i)
        query, places = query_of(k)
        found = against(query, places, k, found_ref[...], True)
        column = jnp.max(found, axis=1, keepdims=True)
        for i in range(2):
            best[2 * core + i, pl.ds(k, 1), :] = to_row(column[i * SLOT:(i + 1) * SLOT])

    def take(k):
        share(k)
        if not isinstance(k, int):
            pl.when(k >= 1)(lambda: compare_same(k - 1))
        elif k >= 1:
            compare_same(k - 1)
        compare_old(k)

    best[...] = jnp.full(best.shape, -1.0, F32)
    for copy in info:
        copy.wait()

    rows, meta = prepare(0)
    recv[0:SLOT] = rows
    meta_recv[0] = meta

    def prepare_step(k, carry):
        rows, meta = prepare(k)
        send[k] = rows
        meta_send[k] = meta
        return carry

    def leave_step(k, carry):
        for copy in x_copies(k):
            copy.start()
        return carry

    lax.fori_loop(1, EARLY, prepare_step, 0)
    pl.semaphore_wait(barrier, 19)
    for step in range(1, 4):
        pl.semaphore_signal(ready, inc=1, device_id=(4 * lax.rem(z + step, 4) + y, g), device_id_type=MESH)
    lax.fori_loop(1, EARLY, leave_step, 0)
    send_first(0)
    lax.fori_loop(EARLY, 8, lambda k, carry: leave_step(k, prepare_step(k, carry)), 0)
    pl.semaphore_wait(ready, 3)

    def pass_on(k, carry):
        for copy in x_copies(k):
            copy.wait_recv()
        send_first(k)
        pl.when(k >= PASS)(lambda: send_second(k - PASS))

        @pl.when(busy & (k >= LAG))
        def _():
            take(k - LAG)

        return carry

    lax.fori_loop(1, 8, pass_on, 0)
    lax.fori_loop(8 - PASS, 8, lambda k, carry: (send_second(k), carry)[1], 0)

    def small(q, carry):
        query = recv[pl.ds(pl.multiple_of(q * 256, 256), 256)]
        labels = jnp.concatenate([to_column(meta_recv[2 * q + i, 0:1, :]) for i in range(2)], axis=0)
        labels = jnp.where(labels < LARGE_IDS, -1.0, labels)
        places = jnp.concatenate([to_column(meta_recv[2 * q + i, 1:2, :]) for i in range(2)], axis=0)
        found = jnp.full((256, SLOT), -1.0, F32)
        for j in range(4):
            scores = product(query, recv[j * 256:(j + 1) * 256])
            for i in range(2):
                match = (meta_recv[2 * j + i, 0:1, :] == labels) & (meta_recv[2 * j + i, 1:2, :] < places)
                found = jnp.maximum(found, jnp.where(match, scores[:, i * SLOT:(i + 1) * SLOT], -1.0))
        column = jnp.max(found, axis=1, keepdims=True)
        for i in range(2):
            small_best[pl.ds(2 * q + i, 1), :] = to_row(column[i * SLOT:(i + 1) * SLOT])
        return carry

    @pl.when(jnp.logical_not(busy))
    def _():
        lax.fori_loop(0, 4, small, 0)

    def result_copies(i):
        spot = 2 * z + core
        return (
            pltpu.make_async_remote_copy(
                tile_send.at[i], large_in.at[spot], ts.at[i], tr.at[spot], (i, 2 * x + host), MESH),
            pltpu.make_async_copy(tile_send.at[i], large_in.at[spot], tr.at[spot]),
        )

    even = lax.rem(iota((8, SLOT), 0), 2) == 0

    @pl.when(busy)
    def _():
        for k in range(8 - LAG, 8):
            take(k)
        compare_same(7)
        for i in range(16):
            tile_send[i] = jnp.where(even, best[i % 4], best[i // 4])
            far, near = result_copies(i)
            mine = (b == i) & (host == core)
            pl.when(jnp.logical_not(mine))(far.start)
            pl.when(mine)(near.start)
        lax.fori_loop(0, 4, small, 0)

    def drain_line(k, carry):
        for copy in x_copies(k):
            copy.wait_send()
        return carry

    lax.fori_loop(1, 8, drain_line, 0)

    def drain_plane(k, carry):
        staged, a, _ = axes(k)

        def piece(step, inner):
            t = lax.rem(a + step, 4)
            for copy in first_copies(k, t):
                copy.wait_send()
            return inner

        lax.fori_loop(1, 4, piece, 0)

        @pl.when(jnp.logical_not(staged | direct_near(a)))
        def _():
            for copy in direct_copies(k, a)[:2]:
                copy.wait_send()

        split, stays = second_kind(k)

        @pl.when(staged & split)
        def _():
            for n in range(2):
                for copy in split_copies(k, n):
                    copy.wait_send()

        @pl.when(staged & jnp.logical_not(split | stays))
        def _():
            for copy in block_copies(k)[:2]:
                copy.wait_send()

        @pl.when(jnp.logical_not(busy))
        def _():
            for copy in turned_copies(k):
                copy.wait_send()

        return carry

    lax.fori_loop(0, 8, drain_plane, 0)

    @pl.when(busy)
    def _():
        def drain_share(k, carry):
            for copy in share_copies(k):
                copy.wait_send()
            return carry

        lax.fori_loop(0, 8, drain_share, 0)
        for i in range(16):
            pl.when(jnp.logical_not((b == i) & (host == core)))(result_copies(i)[0].wait_send)

    lane_of = lax.div(iota((8, SLOT), 1), CAP)
    large = jnp.full((8, SLOT), -1.0, F32)
    for c in range(4):
        for h in range(2):
            pltpu.make_async_copy(large_in.at[2 * c + h], large_in.at[2 * c + h], tr.at[2 * c + h]).wait()
        joined = jnp.maximum(large_in[2 * c], large_in[2 * c + 1])
        from_even = pltpu.roll(joined, lax.rem(CAP * (c - z) + SLOT, SLOT), 1)
        from_odd = pltpu.roll(joined, lax.rem(CAP * (c - y) + SLOT, SLOT), 1)
        large = jnp.where(lane_of == c, jnp.where(even, from_even, from_odd), large)
    for k in range(8):
        row = jnp.where(meta_recv[k, 0:1, :] < LARGE_IDS, large[k:k + 1], small_best[k:k + 1, :])
        final_send[k] = row

    def final_copy(k):
        return pltpu.make_async_remote_copy(
            final_send.at[k], final_recv.at[k], os.at[k], orr.at[k], (b, partner(k)), MESH)

    def final_start(k, carry):
        final_copy(k).start()
        return carry

    lax.fori_loop(1, 8, final_start, 0)
    final_recv[0] = final_send[0]

    def unpermute(k):
        out_ref[pl.ds(partner(k), 1), :] = jnp.sum(
            perms[k] * to_column(final_recv[k]), axis=0, keepdims=True)

    unpermute(0)

    def final_step(k, carry):
        final_copy(k).wait_recv()
        unpermute(k)
        return carry

    lax.fori_loop(1, 8, final_step, 0)

    lax.fori_loop(1, 8, lambda k, carry: (final_copy(k).wait_send(), carry)[1], 0)


def shards(embeddings, cluster_ids, orders):
    dma = pltpu.SemaphoreType.DMA
    vmem = pltpu.VMEM
    out = pl.pallas_call(
        kernel,
        out_shape=jax.ShapeDtypeStruct((8, SLOT), F32),
        in_specs=[pl.BlockSpec(memory_space=pl.ANY)] * 3,
        out_specs=pl.BlockSpec(memory_space=pltpu.VMEM),
        scratch_shapes=[
            vmem((8, SLOT, D), BF16),
            vmem((8, SLOT), jnp.int32),
            vmem((8, SLOT), jnp.int32),
            vmem((8, SLOT, D), BF16),
            vmem((8 * SLOT, D), BF16),
            vmem((8, 8, SLOT), F32),
            vmem((8, 8, SLOT), F32),
            vmem((8, SLOT, SLOT), F32),
            vmem((8, 1, SLOT), F32),
            vmem((8, 5 * CAP, D), BF16),
            vmem((8, 5, 1, SLOT), F32),
            vmem((8, 512, D), BF16),
            vmem((8, 16, 1, SLOT), F32),
            vmem((8, 8, SLOT), F32),
            vmem((4, 8, SLOT), F32),
            vmem((256, SLOT), F32),
            vmem((16, 8, SLOT), F32),
            vmem((8, 8, SLOT), F32),
            vmem((8, SLOT), F32),
            vmem((8, 1, SLOT), F32),
            vmem((8, 1, SLOT), F32),
            dma((8,)), dma((2,)),
            dma((8,)), dma((8,)), dma((8,)), dma((8,)),
            dma((8, 4)), dma((8, 2)), dma((8, 4)), dma((8, 2)),
            dma((8, 2)), dma((8,)), dma((8, 2)), dma((8,)),
            dma((8,)), dma((8,)), dma((8,)), dma((8,)),
            dma((16,)), dma((8,)),
            dma((8,)), dma((8,)),
            pltpu.SemaphoreType.REGULAR,
        ],
        compiler_params=pltpu.CompilerParams(
            collective_id=0, has_side_effects=True, vmem_limit_bytes=60 * 1024 * 1024),
    )(embeddings.reshape(8, SLOT, D), cluster_ids.reshape(8, SLOT), orders.reshape(8, SLOT))
    return out.reshape(1, 1, 8, SLOT)


def solution(mesh):
    in_specs = (
        P("blk", "group", None, None, None),
        P("blk", "group", None, None),
        P("blk", "group", None, None),
    )
    out_specs = P("blk", "group", None, None)
    return jax.shard_map(shards, mesh=mesh, in_specs=in_specs, out_specs=out_specs, check_vma=False)
```

```python
import jax
import jax.numpy as jnp
from jax import lax
from jax.experimental import pallas as pl
from jax.experimental.pallas import tpu as pltpu
from jax.sharding import PartitionSpec as P

MESH = pl.DeviceIdType.MESH
F32 = jnp.float32
BF16 = jnp.bfloat16
D = 768
SLOT = 128
CAP = 32
LARGE_IDS = 32.0
NEVER = 1.0e9
EARLY = 4
ORDER = sum(way << (3 * step) for step, way in enumerate((0, 1, 6, 2, 7, 3, 4, 5)))


def flip(value, bits):
    out = 0
    for shift in (1, 2, 4):
        bit = lax.rem(lax.div(value, shift), 2) + lax.rem(lax.div(bits, shift), 2)
        out = out + shift * lax.rem(bit, 2)
    return out


def iota(shape, dim):
    return lax.broadcasted_iota(jnp.int32, shape, dim)


def to_column(row):
    eye = iota((SLOT, SLOT), 0) == iota((SLOT, SLOT), 1)
    return jnp.sum(jnp.where(eye, jnp.broadcast_to(row, (SLOT, SLOT)), 0.0), axis=1, keepdims=True)


def to_row(column):
    eye = iota((SLOT, SLOT), 0) == iota((SLOT, SLOT), 1)
    return jnp.sum(jnp.where(eye, jnp.broadcast_to(column, (SLOT, SLOT)), 0.0), axis=0, keepdims=True)


def product(query, keys):
    return lax.dot_general(query, keys, (((1,), (1,)), ((), ())), preferred_element_type=F32)


def permutation(ids, group):
    large = ids < LARGE_IDS
    label = jnp.where(large, ids - 4.0 * group.astype(F32), 4.0)
    sub = iota((SLOT, SLOT), 0)
    lane = iota((SLOT, SLOT), 1)
    before = jnp.where((to_column(label) == label) & (sub < lane), 1.0, 0.0)
    rank = jnp.sum(before, axis=0, keepdims=True)
    dest = jnp.where(large, CAP * label + rank, 4096.0)
    subf = sub.astype(F32)
    taken = jnp.where(dest == subf, 1024.0, 0.0) + jnp.where(dest < subf, 1.0, 0.0)
    slot = iota((SLOT, 1), 0).astype(F32)
    free = slot - jnp.sum(taken, axis=1, keepdims=True)
    return jnp.where((dest == subf) | (free == jnp.where(large, -8192.0, rank)), 1.0, 0.0)


def permuted_meta(ids, orders, perm):
    id_high = jnp.floor(ids * (1.0 / 32))
    order_high = jnp.floor(orders * (1.0 / 1024))
    rest = orders - 1024.0 * order_high
    order_mid = jnp.floor(rest * (1.0 / 32))
    at = iota((8, SLOT), 0)
    parts = jnp.zeros((8, SLOT), F32)
    pieces = (id_high, ids - 32.0 * id_high, order_high, order_mid, rest - 32.0 * order_mid)
    for index, piece in enumerate(pieces):
        parts = jnp.where(at == index, jnp.broadcast_to(piece, (8, SLOT)), parts)
    moved = product(parts, perm)
    slot_ids = moved[0:1] * 32.0 + moved[1:2]
    slot_orders = moved[2:3] * 1024.0 + moved[3:4] * 32.0 + moved[4:5]
    large_orders = jnp.where(slot_ids < LARGE_IDS, slot_orders, NEVER)
    out = jnp.where(at == 0, jnp.broadcast_to(slot_ids, (8, SLOT)), jnp.broadcast_to(slot_orders, (8, SLOT)))
    return jnp.where(at == 2, jnp.broadcast_to(large_orders, (8, SLOT)), out)


def kernel(
    emb, ids_in, orders_in, out_ref,
    raw, ids_ref, orders_ref, send, recv, meta_send, meta_recv, perms, plane_meta, mid, mid_meta,
    keys, key_meta, key_orders, best, found_ref, tile_send, large_in, small_best, final_send, final_recv,
    load_sem, info_sem, xs, xr, xms, xmr, ps, pr, pms, pmr, ss, sr, sms, smr, fs, fr, fms, fmr,
    ts, tr, os, orr, ready,
):
    b = lax.axis_index("blk")
    g = lax.axis_index("group")
    z, y = lax.div(b, 4), lax.rem(b, 4)
    x, core = lax.div(g, 2), lax.rem(g, 2)
    offset = lax.rem(y - z + 4, 4)
    busy = lax.rem(offset, 2) == 0
    host = lax.div(offset, 2)

    def relation(k):
        return lax.rem(lax.shift_right_logical(ORDER, 3 * k), 8)

    def partner(k):
        return flip(g, relation(k))

    def load(k):
        return pltpu.make_async_copy(emb.at[partner(k)], raw.at[k], load_sem.at[k])

    info = (
        pltpu.make_async_copy(ids_in, ids_ref, info_sem.at[0]),
        pltpu.make_async_copy(orders_in, orders_ref, info_sem.at[1]),
    )
    for copy in info:
        copy.start()

    def load_step(k, carry):
        load(k).start()
        return carry

    lax.fori_loop(0, 8, load_step, 0)

    barrier = pltpu.get_barrier_semaphore()

    def greet(blk, group):
        pl.semaphore_signal(barrier, inc=1, device_id=(blk, group), device_id_type=MESH)

    for step in range(1, 4):
        for h in range(2):
            greet(4 * lax.rem(z + step, 4) + y, 2 * x + h)
            greet(4 * z + lax.rem(y + step, 4), 2 * x + h)
            greet(b, 2 * lax.rem(x + step, 4) + h)
    greet(b, 2 * x + 1 - core)

    def prepare(k):
        load(k).wait()
        owner = partner(k)
        ids = ids_ref[pl.ds(owner, 1), :].astype(F32)
        orders = orders_ref[pl.ds(owner, 1), :].astype(F32)
        perm = permutation(ids, owner)
        perms[k] = perm
        values = raw[k].astype(F32)
        total = jnp.sum(values * values, axis=1, keepdims=True)
        unit = (values * lax.rsqrt(total + 1e-06)).astype(BF16)
        rows = jnp.dot(perm.astype(BF16), unit, preferred_element_type=F32).astype(BF16)
        return rows, permuted_meta(ids, orders, perm)

    def block_of(k):
        return pl.ds(pl.multiple_of(k * SLOT, SLOT), SLOT)

    def x_copies(k):
        to = (b, partner(k))
        return (
            pltpu.make_async_remote_copy(send.at[k], recv.at[block_of(k)], xs.at[k], xr.at[k], to, MESH),
            pltpu.make_async_remote_copy(meta_send.at[k], meta_recv.at[k], xms.at[k], xmr.at[k], to, MESH),
        )

    def axes(k):
        staged = lax.rem(k, 2) == 0
        return staged, jnp.where(staged, z, y), jnp.where(staged, y, z)

    def device_at(staged, a, bb):
        return jnp.where(staged, 4 * a + bb, 4 * bb + a)

    def first_way(k, t):
        staged, a, bb = axes(k)
        end = lax.rem(t + 2 * core, 4)
        turned = (lax.rem(bb - end + 4, 4) == 2) & (lax.rem(a - t + 4, 2) == 1)
        return turned, device_at(staged, jnp.where(turned, a, t), jnp.where(turned, end, bb))

    def first_copies(k, t):
        staged, a, _ = axes(k)
        turned, stop = first_way(k, t)
        c = jnp.where(staged, t, lax.rem(t + 2 * core, 4))
        at = jnp.where(turned, 4, a)
        which = jnp.where(turned, 1, 0)
        rows = pl.ds(pl.multiple_of(k * SLOT + c * CAP, CAP), CAP)
        spot = pl.ds(pl.multiple_of(at * CAP, CAP), CAP)
        return (
            pltpu.make_async_remote_copy(
                recv.at[rows], mid.at[k, spot], ps.at[k, t], pr.at[k, which], (stop, g), MESH),
            pltpu.make_async_remote_copy(
                plane_meta.at[k], mid_meta.at[k, at], pms.at[k, t], pmr.at[k, which], (stop, g), MESH),
        )

    def first_near(k):
        staged, a, _ = axes(k)
        c = jnp.where(staged, a, lax.rem(a + 2 * core, 4))
        rows = pl.ds(pl.multiple_of(k * SLOT + c * CAP, CAP), CAP)
        spot = pl.ds(pl.multiple_of(a * CAP, CAP), CAP)
        return (
            pltpu.make_async_copy(recv.at[rows], mid.at[k, spot], pr.at[k, 0]),
            pltpu.make_async_copy(plane_meta.at[k], mid_meta.at[k, a], pmr.at[k, 0]),
        )

    def direct_copies(k, t):
        c = lax.rem(t + 2 * core, 4)
        to = (4 * c + t, 2 * x + lax.div(z, 2))
        rows = recv.at[pl.ds(pl.multiple_of(k * SLOT + c * CAP, CAP), CAP)]
        spot = keys.at[k, pl.ds(pl.multiple_of(b * CAP, CAP), CAP)]
        meta, meta_spot = plane_meta.at[k], key_meta.at[k, b]
        return (
            pltpu.make_async_remote_copy(rows, spot, ps.at[k, t], sr.at[k], to, MESH),
            pltpu.make_async_remote_copy(meta, meta_spot, pms.at[k, t], smr.at[k], to, MESH),
            pltpu.make_async_copy(rows, spot, sr.at[k]),
            pltpu.make_async_copy(meta, meta_spot, smr.at[k]),
        )

    def direct_near(t):
        return (4 * lax.rem(t + 2 * core, 4) + t == b) & (lax.div(z, 2) == core)

    def send_first(k):
        plane_meta[k] = meta_recv[k, 2:3, :]
        staged, a, _ = axes(k)

        def piece(step, carry):
            t = lax.rem(a + step, 4)
            turned, _ = first_way(k, t)

            @pl.when(staged | turned)
            def _():
                rows, meta = first_copies(k, t)
                meta.start()
                rows.start()

            @pl.when(jnp.logical_not(staged | turned | direct_near(t)))
            def _():
                rows, meta, _, _ = direct_copies(k, t)
                meta.start()
                rows.start()

            return carry

        lax.fori_loop(1, 4, piece, 0)

        @pl.when(staged)
        def _():
            for copy in first_near(k):
                copy.start()

        @pl.when(jnp.logical_not(staged))
        def _():
            far_rows, far_meta, near_rows, near_meta = direct_copies(k, a)

            @pl.when(direct_near(a))
            def _():
                near_meta.start()
                near_rows.start()

            @pl.when(jnp.logical_not(direct_near(a)))
            def _():
                far_meta.start()
                far_rows.start()

    def piece_copies(k, source, place, blk, sem):
        to = (blk, 2 * x + lax.div(place, 8))
        rows = pl.ds(pl.multiple_of(source * CAP, CAP), CAP)
        spot = pl.ds(pl.multiple_of(place * CAP, CAP), CAP)
        return (
            pltpu.make_async_remote_copy(
                mid.at[k, rows], keys.at[k, spot], ss.at[k, sem], sr.at[k], to, MESH),
            pltpu.make_async_remote_copy(
                mid_meta.at[k, source], key_meta.at[k, place], sms.at[k, sem], smr.at[k], to, MESH),
        )

    def block_copies(k):
        staged, a, bb = axes(k)
        blk = device_at(staged, a, lax.rem(a + 2 * core, 4))
        to = (blk, 2 * x + lax.div(bb, 2))
        rows = mid.at[k, pl.ds(0, SLOT)]
        spot = keys.at[k, pl.ds(pl.multiple_of(bb * SLOT, SLOT), SLOT)]
        meta = mid_meta.at[k, pl.ds(0, 4)]
        meta_spot = key_meta.at[k, pl.ds(pl.multiple_of(bb * 4, 4), 4)]
        return (
            pltpu.make_async_remote_copy(rows, spot, ss.at[k, 0], sr.at[k], to, MESH),
            pltpu.make_async_remote_copy(meta, meta_spot, sms.at[k, 0], smr.at[k], to, MESH),
            pltpu.make_async_copy(rows, spot, sr.at[k]),
            pltpu.make_async_copy(meta, meta_spot, smr.at[k]),
        )

    def second_kind(k):
        _, a, bb = axes(k)
        split = lax.rem(bb - a - 2 * core + 8, 4) == 2
        stays = busy & (host == core) & (lax.div(bb, 2) == core)
        return split, stays

    def split_copies(k, n):
        staged, a, bb = axes(k)
        source = lax.rem(a + 2 * n, 4)
        return piece_copies(k, source, 4 * bb + source, device_at(staged, a, lax.rem(a + 2 * core, 4)), n)

    def turned_copies(k):
        staged, a, bb = axes(k)
        blk = device_at(staged, lax.rem(bb + 2 * core, 4), bb)
        return piece_copies(k, 4, 4 * lax.rem(bb + 2, 4) + a, blk, 1)

    def send_second(k):
        staged, _, _ = axes(k)
        split, stays = second_kind(k)

        @pl.when(staged & split)
        def _():
            half_meta = mid_meta.at[k, pl.ds(0, 2)]
            half_rows = mid.at[k, pl.ds(0, 2 * CAP)]
            pltpu.make_async_copy(half_meta, half_meta, pmr.at[k, 0]).wait()
            pltpu.make_async_copy(half_rows, half_rows, pr.at[k, 0]).wait()
            for n in range(2):
                rows, meta = split_copies(k, n)
                meta.start()
                rows.start()

        @pl.when(staged & jnp.logical_not(split))
        def _():
            all_meta = mid_meta.at[k, pl.ds(0, 4)]
            all_rows = mid.at[k, pl.ds(0, SLOT)]
            pltpu.make_async_copy(all_meta, all_meta, pmr.at[k, 0]).wait()
            pltpu.make_async_copy(all_rows, all_rows, pr.at[k, 0]).wait()
            far_rows, far_meta, near_rows, near_meta = block_copies(k)

            @pl.when(jnp.logical_not(stays))
            def _():
                far_meta.start()
                far_rows.start()

            @pl.when(stays)
            def _():
                near_meta.start()
                near_rows.start()

        @pl.when(jnp.logical_not(busy))
        def _():
            rows, meta = turned_copies(k)
            one_meta = mid_meta.at[k, 4]
            one_rows = mid.at[k, pl.ds(4 * CAP, CAP)]
            pltpu.make_async_copy(one_meta, one_meta, pmr.at[k, 1]).wait()
            pltpu.make_async_copy(one_rows, one_rows, pr.at[k, 1]).wait()
            meta.start()
            rows.start()

    def share_copies(k):
        to = (b, 2 * x + 1 - core)
        rows = pl.ds(pl.multiple_of(core * 256, 256), 256)
        sources = pl.ds(pl.multiple_of(core * 8, 8), 8)
        return (
            pltpu.make_async_remote_copy(keys.at[k, rows], keys.at[k, rows], fs.at[k], fr.at[k], to, MESH),
            pltpu.make_async_remote_copy(
                key_meta.at[k, sources], key_meta.at[k, sources], fms.at[k], fmr.at[k], to, MESH),
        )

    def share(k):
        rows = keys.at[k, pl.ds(pl.multiple_of(core * 256, 256), 256)]
        sources = key_meta.at[k, pl.ds(pl.multiple_of(core * 8, 8), 8)]
        pltpu.make_async_copy(sources, sources, smr.at[k]).wait()
        pltpu.make_async_copy(rows, rows, sr.at[k]).wait()
        for copy in share_copies(k):
            copy.start()

    lane_part = lax.div(iota((1, SLOT), 1), CAP)

    def merge_orders(k, u):
        merged = jnp.zeros((1, SLOT), F32)
        for j in range(4):
            shift = lax.rem(CAP * (j - z) + SLOT, SLOT)
            merged = jnp.where(lane_part == j, pltpu.roll(key_meta[k, 4 * u + j], shift, 1), merged)
        key_orders[k, pl.ds(u, 1), :] = merged

    def query_of(k):
        places = [to_column(key_orders[k, pl.ds(2 * core + i, 1), :]) for i in range(2)]
        return keys[k, pl.ds(pl.multiple_of(core * 256, 256), 256)], jnp.concatenate(places, axis=0)

    def against(query, places, j, found, one_way):
        for h in range(2):
            scores = product(query, keys[j, h * 256:(h + 1) * 256])
            for i in range(2):
                u = 2 * h + i
                part = scores[:, i * SLOT:(i + 1) * SLOT]
                earlier = key_orders[j, u:u + 1, :] < places
                found = jnp.maximum(found, jnp.where(earlier, part, -1.0))
                if not one_way:
                    other = jnp.max(jnp.where(earlier, -1.0, part), axis=0, keepdims=True)
                    best[u, pl.ds(j, 1), :] = jnp.maximum(best[u, pl.ds(j, 1), :], other)
        return found

    def compare_old(k):
        for i in range(2):
            merge_orders(k, 2 * core + i)
        query, places = query_of(k)
        start = jnp.full((256, SLOT), -1.0, F32)
        if isinstance(k, int):
            found = start
            for j in range(k):
                found = against(query, places, j, found, False)
            found_ref[...] = found
            return

        def two(j, found):
            return against(query, places, 2 * j + 1, against(query, places, 2 * j, found, False), False)

        found_ref[...] = lax.fori_loop(0, lax.div(k, 2), two, start)

        @pl.when(lax.rem(k, 2) == 1)
        def _():
            found_ref[...] = against(query, places, k - 1, found_ref[...], False)

    def compare_same(k):
        for copy in share_copies(k):
            copy.wait_recv()
        for i in range(2):
            merge_orders(k, 2 * (1 - core) + i)
        query, places = query_of(k)
        found = against(query, places, k, found_ref[...], True)
        column = jnp.max(found, axis=1, keepdims=True)
        for i in range(2):
            best[2 * core + i, pl.ds(k, 1), :] = to_row(column[i * SLOT:(i + 1) * SLOT])

    def take(k):
        share(k)
        compare_old(k)
        compare_same(k)

    best[...] = jnp.full(best.shape, -1.0, F32)
    for copy in info:
        copy.wait()

    rows, meta = prepare(0)
    recv[0:SLOT] = rows
    meta_recv[0] = meta

    def prepare_step(k, carry):
        rows, meta = prepare(k)
        send[k] = rows
        meta_send[k] = meta
        return carry

    def leave_step(k, carry):
        for copy in x_copies(k):
            copy.start()
        return carry

    def arrive(k):
        for copy in x_copies(k):
            copy.wait_recv()
        send_first(k)

    lax.fori_loop(1, EARLY, prepare_step, 0)
    pl.semaphore_wait(barrier, 19)
    for step in range(1, 4):
        pl.semaphore_signal(ready, inc=1, device_id=(4 * lax.rem(z + step, 4) + y, g), device_id_type=MESH)
    lax.fori_loop(1, EARLY, leave_step, 0)
    send_first(0)
    pl.semaphore_wait(ready, 3)
    arrive(1)
    lax.fori_loop(EARLY, 8, lambda k, carry: leave_step(k, prepare_step(k, carry)), 0)

    arrive(2)
    send_second(0)
    arrive(3)
    send_second(1)
    arrive(4)
    send_second(2)
    pl.when(busy)(lambda: take(0))
    arrive(5)
    send_second(3)
    pl.when(busy)(lambda: take(1))
    arrive(6)
    send_second(4)
    pl.when(busy)(lambda: take(2))
    arrive(7)
    send_second(5)
    pl.when(busy)(lambda: take(3))
    send_second(6)
    send_second(7)

    def small(q, carry):
        query = recv[pl.ds(pl.multiple_of(q * 256, 256), 256)]
        labels = jnp.concatenate([to_column(meta_recv[2 * q + i, 0:1, :]) for i in range(2)], axis=0)
        labels = jnp.where(labels < LARGE_IDS, -1.0, labels)
        places = jnp.concatenate([to_column(meta_recv[2 * q + i, 1:2, :]) for i in range(2)], axis=0)
        found = jnp.full((256, SLOT), -1.0, F32)
        for j in range(4):
            scores = product(query, recv[j * 256:(j + 1) * 256])
            for i in range(2):
                match = (meta_recv[2 * j + i, 0:1, :] == labels) & (meta_recv[2 * j + i, 1:2, :] < places)
                found = jnp.maximum(found, jnp.where(match, scores[:, i * SLOT:(i + 1) * SLOT], -1.0))
        column = jnp.max(found, axis=1, keepdims=True)
        for i in range(2):
            small_best[pl.ds(2 * q + i, 1), :] = to_row(column[i * SLOT:(i + 1) * SLOT])
        return carry

    @pl.when(jnp.logical_not(busy))
    def _():
        lax.fori_loop(0, 4, small, 0)

    def result_copies(i):
        spot = 2 * z + core
        return (
            pltpu.make_async_remote_copy(
                tile_send.at[i], large_in.at[spot], ts.at[i], tr.at[spot], (i, 2 * x + host), MESH),
            pltpu.make_async_copy(tile_send.at[i], large_in.at[spot], tr.at[spot]),
        )

    even = lax.rem(iota((8, SLOT), 0), 2) == 0

    @pl.when(busy)
    def _():
        for k in range(4, 8):
            take(k)
        for i in range(16):
            tile_send[i] = jnp.where(even, best[i % 4], best[i // 4])
            far, near = result_copies(i)
            mine = (b == i) & (host == core)
            pl.when(jnp.logical_not(mine))(far.start)
            pl.when(mine)(near.start)
        lax.fori_loop(0, 4, small, 0)

    lane_of = lax.div(iota((8, SLOT), 1), CAP)
    large = jnp.full((8, SLOT), -1.0, F32)
    for c in range(4):
        for h in range(2):
            pltpu.make_async_copy(large_in.at[2 * c + h], large_in.at[2 * c + h], tr.at[2 * c + h]).wait()
        joined = jnp.maximum(large_in[2 * c], large_in[2 * c + 1])
        from_even = pltpu.roll(joined, lax.rem(CAP * (c - z) + SLOT, SLOT), 1)
        from_odd = pltpu.roll(joined, lax.rem(CAP * (c - y) + SLOT, SLOT), 1)
        large = jnp.where(lane_of == c, jnp.where(even, from_even, from_odd), large)
    for k in range(8):
        row = jnp.where(meta_recv[k, 0:1, :] < LARGE_IDS, large[k:k + 1], small_best[k:k + 1, :])
        final_send[k] = row

    def final_copy(k):
        return pltpu.make_async_remote_copy(
            final_send.at[k], final_recv.at[k], os.at[k], orr.at[k], (b, partner(k)), MESH)

    def final_start(k, carry):
        final_copy(k).start()
        return carry

    lax.fori_loop(1, 8, final_start, 0)
    def drain_line(k, carry):
        for copy in x_copies(k):
            copy.wait_send()
        return carry

    lax.fori_loop(1, 8, drain_line, 0)

    def drain_plane(k, carry):
        staged, a, _ = axes(k)

        def piece(step, inner):
            t = lax.rem(a + step, 4)
            for copy in first_copies(k, t):
                copy.wait_send()
            return inner

        lax.fori_loop(1, 4, piece, 0)

        @pl.when(jnp.logical_not(staged | direct_near(a)))
        def _():
            for copy in direct_copies(k, a)[:2]:
                copy.wait_send()

        split, stays = second_kind(k)

        @pl.when(staged & split)
        def _():
            for n in range(2):
                for copy in split_copies(k, n):
                    copy.wait_send()

        @pl.when(staged & jnp.logical_not(split | stays))
        def _():
            for copy in block_copies(k)[:2]:
                copy.wait_send()

        @pl.when(jnp.logical_not(busy))
        def _():
            for copy in turned_copies(k):
                copy.wait_send()

        return carry

    lax.fori_loop(0, 8, drain_plane, 0)

    @pl.when(busy)
    def _():
        def drain_share(k, carry):
            for copy in share_copies(k):
                copy.wait_send()
            return carry

        lax.fori_loop(0, 8, drain_share, 0)
        for i in range(16):
            pl.when(jnp.logical_not((b == i) & (host == core)))(result_copies(i)[0].wait_send)

    final_recv[0] = final_send[0]

    def unpermute(k):
        out_ref[pl.ds(partner(k), 1), :] = jnp.sum(
            perms[k] * to_column(final_recv[k]), axis=0, keepdims=True)

    unpermute(0)

    def final_step(k, carry):
        final_copy(k).wait_recv()
        unpermute(k)
        return carry

    lax.fori_loop(1, 8, final_step, 0)

    lax.fori_loop(1, 8, lambda k, carry: (final_copy(k).wait_send(), carry)[1], 0)


def shards(embeddings, cluster_ids, orders):
    dma = pltpu.SemaphoreType.DMA
    vmem = pltpu.VMEM
    out = pl.pallas_call(
        kernel,
        out_shape=jax.ShapeDtypeStruct((8, SLOT), F32),
        in_specs=[pl.BlockSpec(memory_space=pl.ANY)] * 3,
        out_specs=pl.BlockSpec(memory_space=pltpu.VMEM),
        scratch_shapes=[
            vmem((8, SLOT, D), BF16),
            vmem((8, SLOT), jnp.int32),
            vmem((8, SLOT), jnp.int32),
            vmem((8, SLOT, D), BF16),
            vmem((8 * SLOT, D), BF16),
            vmem((8, 8, SLOT), F32),
            vmem((8, 8, SLOT), F32),
            vmem((8, SLOT, SLOT), F32),
            vmem((8, 1, SLOT), F32),
            vmem((8, 5 * CAP, D), BF16),
            vmem((8, 5, 1, SLOT), F32),
            vmem((8, 512, D), BF16),
            vmem((8, 16, 1, SLOT), F32),
            vmem((8, 8, SLOT), F32),
            vmem((4, 8, SLOT), F32),
            vmem((256, SLOT), F32),
            vmem((16, 8, SLOT), F32),
            vmem((8, 8, SLOT), F32),
            vmem((8, SLOT), F32),
            vmem((8, 1, SLOT), F32),
            vmem((8, 1, SLOT), F32),
            dma((8,)), dma((2,)),
            dma((8,)), dma((8,)), dma((8,)), dma((8,)),
            dma((8, 4)), dma((8, 2)), dma((8, 4)), dma((8, 2)),
            dma((8, 2)), dma((8,)), dma((8, 2)), dma((8,)),
            dma((8,)), dma((8,)), dma((8,)), dma((8,)),
            dma((16,)), dma((8,)),
            dma((8,)), dma((8,)),
            pltpu.SemaphoreType.REGULAR,
        ],
        compiler_params=pltpu.CompilerParams(
            collective_id=0, has_side_effects=True, vmem_limit_bytes=60 * 1024 * 1024),
    )(embeddings.reshape(8, SLOT, D), cluster_ids.reshape(8, SLOT), orders.reshape(8, SLOT))
    return out.reshape(1, 1, 8, SLOT)


def solution(mesh):
    in_specs = (
        P("blk", "group", None, None, None),
        P("blk", "group", None, None),
        P("blk", "group", None, None),
    )
    out_specs = P("blk", "group", None, None)
    return jax.shard_map(shards, mesh=mesh, in_specs=in_specs, out_specs=out_specs, check_vma=False)
```

```python
import jax
import jax.numpy as jnp
from jax import lax
from jax.experimental import pallas as pl
from jax.experimental.pallas import tpu as pltpu
from jax.sharding import PartitionSpec as P

MESH = pl.DeviceIdType.MESH
F32 = jnp.float32
BF16 = jnp.bfloat16
D = 768
SLOT = 128
CAP = 32
LARGE_IDS = 32.0
NEVER = 1.0e9
EARLY = 5
ORDER = sum(way << (3 * step) for step, way in enumerate((0, 1, 6, 2, 7, 3, 4, 5)))


def flip(value, bits):
    out = 0
    for shift in (1, 2, 4):
        bit = lax.rem(lax.div(value, shift), 2) + lax.rem(lax.div(bits, shift), 2)
        out = out + shift * lax.rem(bit, 2)
    return out


def iota(shape, dim):
    return lax.broadcasted_iota(jnp.int32, shape, dim)


def to_column(row):
    eye = iota((SLOT, SLOT), 0) == iota((SLOT, SLOT), 1)
    return jnp.sum(jnp.where(eye, jnp.broadcast_to(row, (SLOT, SLOT)), 0.0), axis=1, keepdims=True)


def to_row(column):
    eye = iota((SLOT, SLOT), 0) == iota((SLOT, SLOT), 1)
    return jnp.sum(jnp.where(eye, jnp.broadcast_to(column, (SLOT, SLOT)), 0.0), axis=0, keepdims=True)


def product(query, keys):
    return lax.dot_general(query, keys, (((1,), (1,)), ((), ())), preferred_element_type=F32)


def permutation(ids, group):
    large = ids < LARGE_IDS
    label = jnp.where(large, ids - 4.0 * group.astype(F32), 4.0)
    sub = iota((SLOT, SLOT), 0)
    lane = iota((SLOT, SLOT), 1)
    before = jnp.where((to_column(label) == label) & (sub < lane), 1.0, 0.0)
    rank = jnp.sum(before, axis=0, keepdims=True)
    dest = jnp.where(large, CAP * label + rank, 4096.0)
    subf = sub.astype(F32)
    taken = jnp.where(dest == subf, 1024.0, 0.0) + jnp.where(dest < subf, 1.0, 0.0)
    slot = iota((SLOT, 1), 0).astype(F32)
    free = slot - jnp.sum(taken, axis=1, keepdims=True)
    return jnp.where((dest == subf) | (free == jnp.where(large, -8192.0, rank)), 1.0, 0.0)


def permuted_meta(ids, orders, perm):
    id_high = jnp.floor(ids * (1.0 / 32))
    order_high = jnp.floor(orders * (1.0 / 1024))
    rest = orders - 1024.0 * order_high
    order_mid = jnp.floor(rest * (1.0 / 32))
    at = iota((8, SLOT), 0)
    parts = jnp.zeros((8, SLOT), F32)
    pieces = (id_high, ids - 32.0 * id_high, order_high, order_mid, rest - 32.0 * order_mid)
    for index, piece in enumerate(pieces):
        parts = jnp.where(at == index, jnp.broadcast_to(piece, (8, SLOT)), parts)
    moved = product(parts, perm)
    slot_ids = moved[0:1] * 32.0 + moved[1:2]
    slot_orders = moved[2:3] * 1024.0 + moved[3:4] * 32.0 + moved[4:5]
    large_orders = jnp.where(slot_ids < LARGE_IDS, slot_orders, NEVER)
    out = jnp.where(at == 0, jnp.broadcast_to(slot_ids, (8, SLOT)), jnp.broadcast_to(slot_orders, (8, SLOT)))
    return jnp.where(at == 2, jnp.broadcast_to(large_orders, (8, SLOT)), out)


def kernel(
    emb, ids_in, orders_in, out_ref,
    raw, ids_ref, orders_ref, send, recv, meta_send, meta_recv, perms, plane_meta, mid, mid_meta,
    keys, key_meta, key_orders, best, found_ref, tile_send, large_in, small_best, final_send, final_recv,
    load_sem, info_sem, xs, xr, xms, xmr, ps, pr, pms, pmr, ss, sr, sms, smr, fs, fr, fms, fmr,
    ts, tr, os, orr, ready,
):
    b = lax.axis_index("blk")
    g = lax.axis_index("group")
    z, y = lax.div(b, 4), lax.rem(b, 4)
    x, core = lax.div(g, 2), lax.rem(g, 2)
    offset = lax.rem(y - z + 4, 4)
    busy = lax.rem(offset, 2) == 0
    host = lax.div(offset, 2)

    def relation(k):
        return lax.rem(lax.shift_right_logical(ORDER, 3 * k), 8)

    def partner(k):
        return flip(g, relation(k))

    def load(k):
        return pltpu.make_async_copy(emb.at[partner(k)], raw.at[k], load_sem.at[k])

    info = (
        pltpu.make_async_copy(ids_in, ids_ref, info_sem.at[0]),
        pltpu.make_async_copy(orders_in, orders_ref, info_sem.at[1]),
    )
    for copy in info:
        copy.start()

    def load_step(k, carry):
        load(k).start()
        return carry

    lax.fori_loop(0, 8, load_step, 0)

    barrier = pltpu.get_barrier_semaphore()

    def greet(blk, group):
        pl.semaphore_signal(barrier, inc=1, device_id=(blk, group), device_id_type=MESH)

    for step in range(1, 4):
        for h in range(2):
            greet(4 * lax.rem(z + step, 4) + y, 2 * x + h)
            greet(4 * z + lax.rem(y + step, 4), 2 * x + h)
            greet(b, 2 * lax.rem(x + step, 4) + h)
    greet(b, 2 * x + 1 - core)

    def prepare(k):
        load(k).wait()
        owner = partner(k)
        ids = ids_ref[pl.ds(owner, 1), :].astype(F32)
        orders = orders_ref[pl.ds(owner, 1), :].astype(F32)
        perm = permutation(ids, owner)
        perms[k] = perm
        values = raw[k].astype(F32)
        total = jnp.sum(values * values, axis=1, keepdims=True)
        unit = (values * lax.rsqrt(total + 1e-06)).astype(BF16)
        rows = jnp.dot(perm.astype(BF16), unit, preferred_element_type=F32).astype(BF16)
        return rows, permuted_meta(ids, orders, perm)

    def block_of(k):
        return pl.ds(pl.multiple_of(k * SLOT, SLOT), SLOT)

    def x_copies(k):
        to = (b, partner(k))
        return (
            pltpu.make_async_remote_copy(send.at[k], recv.at[block_of(k)], xs.at[k], xr.at[k], to, MESH),
            pltpu.make_async_remote_copy(meta_send.at[k], meta_recv.at[k], xms.at[k], xmr.at[k], to, MESH),
        )

    def axes(k):
        staged = lax.rem(k, 2) == 0
        return staged, jnp.where(staged, z, y), jnp.where(staged, y, z)

    def device_at(staged, a, bb):
        return jnp.where(staged, 4 * a + bb, 4 * bb + a)

    def first_way(k, t):
        staged, a, bb = axes(k)
        end = lax.rem(t + 2 * core, 4)
        turned = (lax.rem(bb - end + 4, 4) == 2) & (lax.rem(a - t + 4, 2) == 1)
        return turned, device_at(staged, jnp.where(turned, a, t), jnp.where(turned, end, bb))

    def first_copies(k, t):
        staged, a, _ = axes(k)
        turned, stop = first_way(k, t)
        c = jnp.where(staged, t, lax.rem(t + 2 * core, 4))
        at = jnp.where(turned, 4, a)
        which = jnp.where(turned, 1, 0)
        rows = pl.ds(pl.multiple_of(k * SLOT + c * CAP, CAP), CAP)
        spot = pl.ds(pl.multiple_of(at * CAP, CAP), CAP)
        return (
            pltpu.make_async_remote_copy(
                recv.at[rows], mid.at[k, spot], ps.at[k, t], pr.at[k, which], (stop, g), MESH),
            pltpu.make_async_remote_copy(
                plane_meta.at[k], mid_meta.at[k, at], pms.at[k, t], pmr.at[k, which], (stop, g), MESH),
        )

    def first_near(k):
        staged, a, _ = axes(k)
        c = jnp.where(staged, a, lax.rem(a + 2 * core, 4))
        rows = pl.ds(pl.multiple_of(k * SLOT + c * CAP, CAP), CAP)
        spot = pl.ds(pl.multiple_of(a * CAP, CAP), CAP)
        return (
            pltpu.make_async_copy(recv.at[rows], mid.at[k, spot], pr.at[k, 0]),
            pltpu.make_async_copy(plane_meta.at[k], mid_meta.at[k, a], pmr.at[k, 0]),
        )

    def direct_copies(k, t):
        c = lax.rem(t + 2 * core, 4)
        to = (4 * c + t, 2 * x + lax.div(z, 2))
        rows = recv.at[pl.ds(pl.multiple_of(k * SLOT + c * CAP, CAP), CAP)]
        spot = keys.at[k, pl.ds(pl.multiple_of(b * CAP, CAP), CAP)]
        meta, meta_spot = plane_meta.at[k], key_meta.at[k, b]
        return (
            pltpu.make_async_remote_copy(rows, spot, ps.at[k, t], sr.at[k], to, MESH),
            pltpu.make_async_remote_copy(meta, meta_spot, pms.at[k, t], smr.at[k], to, MESH),
            pltpu.make_async_copy(rows, spot, sr.at[k]),
            pltpu.make_async_copy(meta, meta_spot, smr.at[k]),
        )

    def direct_near(t):
        return (4 * lax.rem(t + 2 * core, 4) + t == b) & (lax.div(z, 2) == core)

    def send_first(k):
        plane_meta[k] = meta_recv[k, 2:3, :]
        staged, a, _ = axes(k)

        def piece(step, carry):
            t = lax.rem(a + step, 4)
            turned, _ = first_way(k, t)

            @pl.when(staged | turned)
            def _():
                rows, meta = first_copies(k, t)
                meta.start()
                rows.start()

            @pl.when(jnp.logical_not(staged | turned | direct_near(t)))
            def _():
                rows, meta, _, _ = direct_copies(k, t)
                meta.start()
                rows.start()

            return carry

        lax.fori_loop(1, 4, piece, 0)

        @pl.when(staged)
        def _():
            for copy in first_near(k):
                copy.start()

        @pl.when(jnp.logical_not(staged))
        def _():
            far_rows, far_meta, near_rows, near_meta = direct_copies(k, a)

            @pl.when(direct_near(a))
            def _():
                near_meta.start()
                near_rows.start()

            @pl.when(jnp.logical_not(direct_near(a)))
            def _():
                far_meta.start()
                far_rows.start()

    def piece_copies(k, source, place, blk, sem):
        to = (blk, 2 * x + lax.div(place, 8))
        rows = pl.ds(pl.multiple_of(source * CAP, CAP), CAP)
        spot = pl.ds(pl.multiple_of(place * CAP, CAP), CAP)
        return (
            pltpu.make_async_remote_copy(
                mid.at[k, rows], keys.at[k, spot], ss.at[k, sem], sr.at[k], to, MESH),
            pltpu.make_async_remote_copy(
                mid_meta.at[k, source], key_meta.at[k, place], sms.at[k, sem], smr.at[k], to, MESH),
        )

    def block_copies(k):
        staged, a, bb = axes(k)
        blk = device_at(staged, a, lax.rem(a + 2 * core, 4))
        to = (blk, 2 * x + lax.div(bb, 2))
        rows = mid.at[k, pl.ds(0, SLOT)]
        spot = keys.at[k, pl.ds(pl.multiple_of(bb * SLOT, SLOT), SLOT)]
        meta = mid_meta.at[k, pl.ds(0, 4)]
        meta_spot = key_meta.at[k, pl.ds(pl.multiple_of(bb * 4, 4), 4)]
        return (
            pltpu.make_async_remote_copy(rows, spot, ss.at[k, 0], sr.at[k], to, MESH),
            pltpu.make_async_remote_copy(meta, meta_spot, sms.at[k, 0], smr.at[k], to, MESH),
            pltpu.make_async_copy(rows, spot, sr.at[k]),
            pltpu.make_async_copy(meta, meta_spot, smr.at[k]),
        )

    def second_kind(k):
        _, a, bb = axes(k)
        split = lax.rem(bb - a - 2 * core + 8, 4) == 2
        stays = busy & (host == core) & (lax.div(bb, 2) == core)
        return split, stays

    def split_copies(k, n):
        staged, a, bb = axes(k)
        source = lax.rem(a + 2 * n, 4)
        return piece_copies(k, source, 4 * bb + source, device_at(staged, a, lax.rem(a + 2 * core, 4)), n)

    def turned_copies(k):
        staged, a, bb = axes(k)
        blk = device_at(staged, lax.rem(bb + 2 * core, 4), bb)
        return piece_copies(k, 4, 4 * lax.rem(bb + 2, 4) + a, blk, 1)

    def send_second(k):
        staged, _, _ = axes(k)
        split, stays = second_kind(k)

        @pl.when(staged & split)
        def _():
            half_meta = mid_meta.at[k, pl.ds(0, 2)]
            half_rows = mid.at[k, pl.ds(0, 2 * CAP)]
            pltpu.make_async_copy(half_meta, half_meta, pmr.at[k, 0]).wait()
            pltpu.make_async_copy(half_rows, half_rows, pr.at[k, 0]).wait()
            for n in range(2):
                rows, meta = split_copies(k, n)
                meta.start()
                rows.start()

        @pl.when(staged & jnp.logical_not(split))
        def _():
            all_meta = mid_meta.at[k, pl.ds(0, 4)]
            all_rows = mid.at[k, pl.ds(0, SLOT)]
            pltpu.make_async_copy(all_meta, all_meta, pmr.at[k, 0]).wait()
            pltpu.make_async_copy(all_rows, all_rows, pr.at[k, 0]).wait()
            far_rows, far_meta, near_rows, near_meta = block_copies(k)

            @pl.when(jnp.logical_not(stays))
            def _():
                far_meta.start()
                far_rows.start()

            @pl.when(stays)
            def _():
                near_meta.start()
                near_rows.start()

        @pl.when(jnp.logical_not(busy))
        def _():
            rows, meta = turned_copies(k)
            one_meta = mid_meta.at[k, 4]
            one_rows = mid.at[k, pl.ds(4 * CAP, CAP)]
            pltpu.make_async_copy(one_meta, one_meta, pmr.at[k, 1]).wait()
            pltpu.make_async_copy(one_rows, one_rows, pr.at[k, 1]).wait()
            meta.start()
            rows.start()

    def share_copies(k):
        to = (b, 2 * x + 1 - core)
        rows = pl.ds(pl.multiple_of(core * 256, 256), 256)
        sources = pl.ds(pl.multiple_of(core * 8, 8), 8)
        return (
            pltpu.make_async_remote_copy(keys.at[k, rows], keys.at[k, rows], fs.at[k], fr.at[k], to, MESH),
            pltpu.make_async_remote_copy(
                key_meta.at[k, sources], key_meta.at[k, sources], fms.at[k], fmr.at[k], to, MESH),
        )

    def share(k):
        rows = keys.at[k, pl.ds(pl.multiple_of(core * 256, 256), 256)]
        sources = key_meta.at[k, pl.ds(pl.multiple_of(core * 8, 8), 8)]
        pltpu.make_async_copy(sources, sources, smr.at[k]).wait()
        pltpu.make_async_copy(rows, rows, sr.at[k]).wait()
        for copy in share_copies(k):
            copy.start()

    lane_part = lax.div(iota((1, SLOT), 1), CAP)

    def merge_orders(k, u):
        merged = jnp.zeros((1, SLOT), F32)
        for j in range(4):
            shift = lax.rem(CAP * (j - z) + SLOT, SLOT)
            merged = jnp.where(lane_part == j, pltpu.roll(key_meta[k, 4 * u + j], shift, 1), merged)
        key_orders[k, pl.ds(u, 1), :] = merged

    def query_of(k):
        places = [to_column(key_orders[k, pl.ds(2 * core + i, 1), :]) for i in range(2)]
        return keys[k, pl.ds(pl.multiple_of(core * 256, 256), 256)], jnp.concatenate(places, axis=0)

    def against(query, places, j, found, one_way):
        for h in range(2):
            scores = product(query, keys[j, h * 256:(h + 1) * 256])
            for i in range(2):
                u = 2 * h + i
                part = scores[:, i * SLOT:(i + 1) * SLOT]
                earlier = key_orders[j, u:u + 1, :] < places
                found = jnp.maximum(found, jnp.where(earlier, part, -1.0))
                if not one_way:
                    other = jnp.max(jnp.where(earlier, -1.0, part), axis=0, keepdims=True)
                    best[u, pl.ds(j, 1), :] = jnp.maximum(best[u, pl.ds(j, 1), :], other)
        return found

    def compare_old(k):
        for i in range(2):
            merge_orders(k, 2 * core + i)
        query, places = query_of(k)
        start = jnp.full((256, SLOT), -1.0, F32)
        if isinstance(k, int):
            found = start
            for j in range(k):
                found = against(query, places, j, found, False)
            found_ref[...] = found
            return

        def two(j, found):
            return against(query, places, 2 * j + 1, against(query, places, 2 * j, found, False), False)

        found_ref[...] = lax.fori_loop(0, lax.div(k, 2), two, start)

        @pl.when(lax.rem(k, 2) == 1)
        def _():
            found_ref[...] = against(query, places, k - 1, found_ref[...], False)

    def compare_same(k):
        for copy in share_copies(k):
            copy.wait_recv()
        for i in range(2):
            merge_orders(k, 2 * (1 - core) + i)
        query, places = query_of(k)
        found = against(query, places, k, found_ref[...], True)
        column = jnp.max(found, axis=1, keepdims=True)
        for i in range(2):
            best[2 * core + i, pl.ds(k, 1), :] = to_row(column[i * SLOT:(i + 1) * SLOT])

    def take(k):
        share(k)
        compare_old(k)
        compare_same(k)

    best[...] = jnp.full(best.shape, -1.0, F32)
    for copy in info:
        copy.wait()

    rows, meta = prepare(0)
    recv[0:SLOT] = rows
    meta_recv[0] = meta

    def prepare_step(k, carry):
        rows, meta = prepare(k)
        send[k] = rows
        meta_send[k] = meta
        return carry

    def leave_step(k, carry):
        for copy in x_copies(k):
            copy.start()
        return carry

    def arrive(k):
        for copy in x_copies(k):
            copy.wait_recv()
        send_first(k)

    lax.fori_loop(1, EARLY, prepare_step, 0)
    pl.semaphore_wait(barrier, 19)
    for step in range(1, 4):
        pl.semaphore_signal(ready, inc=1, device_id=(4 * lax.rem(z + step, 4) + y, g), device_id_type=MESH)
    lax.fori_loop(1, EARLY, leave_step, 0)
    send_first(0)
    pl.semaphore_wait(ready, 3)
    arrive(1)
    lax.fori_loop(EARLY, 8, lambda k, carry: leave_step(k, prepare_step(k, carry)), 0)

    arrive(2)
    send_second(0)
    arrive(3)
    send_second(1)
    arrive(4)
    send_second(2)
    pl.when(busy)(lambda: take(0))
    arrive(5)
    send_second(3)
    pl.when(busy)(lambda: take(1))
    arrive(6)
    send_second(4)
    pl.when(busy)(lambda: take(2))
    arrive(7)
    send_second(5)
    send_second(6)
    pl.when(busy)(lambda: take(3))
    send_second(7)

    def small(q, carry):
        query = recv[pl.ds(pl.multiple_of(q * 256, 256), 256)]
        labels = jnp.concatenate([to_column(meta_recv[2 * q + i, 0:1, :]) for i in range(2)], axis=0)
        labels = jnp.where(labels < LARGE_IDS, -1.0, labels)
        places = jnp.concatenate([to_column(meta_recv[2 * q + i, 1:2, :]) for i in range(2)], axis=0)
        found = jnp.full((256, SLOT), -1.0, F32)
        for j in range(4):
            scores = product(query, recv[j * 256:(j + 1) * 256])
            for i in range(2):
                match = (meta_recv[2 * j + i, 0:1, :] == labels) & (meta_recv[2 * j + i, 1:2, :] < places)
                found = jnp.maximum(found, jnp.where(match, scores[:, i * SLOT:(i + 1) * SLOT], -1.0))
        column = jnp.max(found, axis=1, keepdims=True)
        for i in range(2):
            small_best[pl.ds(2 * q + i, 1), :] = to_row(column[i * SLOT:(i + 1) * SLOT])
        return carry

    @pl.when(jnp.logical_not(busy))
    def _():
        lax.fori_loop(0, 4, small, 0)

    def result_copies(i):
        spot = 2 * z + core
        return (
            pltpu.make_async_remote_copy(
                tile_send.at[i], large_in.at[spot], ts.at[i], tr.at[spot], (i, 2 * x + host), MESH),
            pltpu.make_async_copy(tile_send.at[i], large_in.at[spot], tr.at[spot]),
        )

    even = lax.rem(iota((8, SLOT), 0), 2) == 0

    @pl.when(busy)
    def _():
        for k in range(4, 8):
            take(k)
        for i in range(16):
            tile_send[i] = jnp.where(even, best[i % 4], best[i // 4])
            far, near = result_copies(i)
            mine = (b == i) & (host == core)
            pl.when(jnp.logical_not(mine))(far.start)
            pl.when(mine)(near.start)
        lax.fori_loop(0, 4, small, 0)

    lane_of = lax.div(iota((8, SLOT), 1), CAP)
    large = jnp.full((8, SLOT), -1.0, F32)
    for c in range(4):
        for h in range(2):
            pltpu.make_async_copy(large_in.at[2 * c + h], large_in.at[2 * c + h], tr.at[2 * c + h]).wait()
        joined = jnp.maximum(large_in[2 * c], large_in[2 * c + 1])
        from_even = pltpu.roll(joined, lax.rem(CAP * (c - z) + SLOT, SLOT), 1)
        from_odd = pltpu.roll(joined, lax.rem(CAP * (c - y) + SLOT, SLOT), 1)
        large = jnp.where(lane_of == c, jnp.where(even, from_even, from_odd), large)
    for k in range(8):
        row = jnp.where(meta_recv[k, 0:1, :] < LARGE_IDS, large[k:k + 1], small_best[k:k + 1, :])
        final_send[k] = row

    def final_copy(k):
        return pltpu.make_async_remote_copy(
            final_send.at[k], final_recv.at[k], os.at[k], orr.at[k], (b, partner(k)), MESH)

    def final_start(k, carry):
        final_copy(k).start()
        return carry

    lax.fori_loop(1, 8, final_start, 0)
    def drain_line(k, carry):
        for copy in x_copies(k):
            copy.wait_send()
        return carry

    lax.fori_loop(1, 8, drain_line, 0)

    def drain_plane(k, carry):
        staged, a, _ = axes(k)

        def piece(step, inner):
            t = lax.rem(a + step, 4)
            for copy in first_copies(k, t):
                copy.wait_send()
            return inner

        lax.fori_loop(1, 4, piece, 0)

        @pl.when(jnp.logical_not(staged | direct_near(a)))
        def _():
            for copy in direct_copies(k, a)[:2]:
                copy.wait_send()

        split, stays = second_kind(k)

        @pl.when(staged & split)
        def _():
            for n in range(2):
                for copy in split_copies(k, n):
                    copy.wait_send()

        @pl.when(staged & jnp.logical_not(split | stays))
        def _():
            for copy in block_copies(k)[:2]:
                copy.wait_send()

        @pl.when(jnp.logical_not(busy))
        def _():
            for copy in turned_copies(k):
                copy.wait_send()

        return carry

    lax.fori_loop(0, 8, drain_plane, 0)

    @pl.when(busy)
    def _():
        def drain_share(k, carry):
            for copy in share_copies(k):
                copy.wait_send()
            return carry

        lax.fori_loop(0, 8, drain_share, 0)
        for i in range(16):
            pl.when(jnp.logical_not((b == i) & (host == core)))(result_copies(i)[0].wait_send)

    final_recv[0] = final_send[0]

    def unpermute(k):
        out_ref[pl.ds(partner(k), 1), :] = jnp.sum(
            perms[k] * to_column(final_recv[k]), axis=0, keepdims=True)

    unpermute(0)

    def final_step(k, carry):
        final_copy(k).wait_recv()
        unpermute(k)
        return carry

    lax.fori_loop(1, 8, final_step, 0)

    lax.fori_loop(1, 8, lambda k, carry: (final_copy(k).wait_send(), carry)[1], 0)


def shards(embeddings, cluster_ids, orders):
    dma = pltpu.SemaphoreType.DMA
    vmem = pltpu.VMEM
    out = pl.pallas_call(
        kernel,
        out_shape=jax.ShapeDtypeStruct((8, SLOT), F32),
        in_specs=[pl.BlockSpec(memory_space=pl.ANY)] * 3,
        out_specs=pl.BlockSpec(memory_space=pltpu.VMEM),
        scratch_shapes=[
            vmem((8, SLOT, D), BF16),
            vmem((8, SLOT), jnp.int32),
            vmem((8, SLOT), jnp.int32),
            vmem((8, SLOT, D), BF16),
            vmem((8 * SLOT, D), BF16),
            vmem((8, 8, SLOT), F32),
            vmem((8, 8, SLOT), F32),
            vmem((8, SLOT, SLOT), F32),
            vmem((8, 1, SLOT), F32),
            vmem((8, 5 * CAP, D), BF16),
            vmem((8, 5, 1, SLOT), F32),
            vmem((8, 512, D), BF16),
            vmem((8, 16, 1, SLOT), F32),
            vmem((8, 8, SLOT), F32),
            vmem((4, 8, SLOT), F32),
            vmem((256, SLOT), F32),
            vmem((16, 8, SLOT), F32),
            vmem((8, 8, SLOT), F32),
            vmem((8, SLOT), F32),
            vmem((8, 1, SLOT), F32),
            vmem((8, 1, SLOT), F32),
            dma((8,)), dma((2,)),
            dma((8,)), dma((8,)), dma((8,)), dma((8,)),
            dma((8, 4)), dma((8, 2)), dma((8, 4)), dma((8, 2)),
            dma((8, 2)), dma((8,)), dma((8, 2)), dma((8,)),
            dma((8,)), dma((8,)), dma((8,)), dma((8,)),
            dma((16,)), dma((8,)),
            dma((8,)), dma((8,)),
            pltpu.SemaphoreType.REGULAR,
        ],
        compiler_params=pltpu.CompilerParams(
            collective_id=0, has_side_effects=True, vmem_limit_bytes=60 * 1024 * 1024),
    )(embeddings.reshape(8, SLOT, D), cluster_ids.reshape(8, SLOT), orders.reshape(8, SLOT))
    return out.reshape(1, 1, 8, SLOT)


def solution(mesh):
    in_specs = (
        P("blk", "group", None, None, None),
        P("blk", "group", None, None),
        P("blk", "group", None, None),
    )
    out_specs = P("blk", "group", None, None)
    return jax.shard_map(shards, mesh=mesh, in_specs=in_specs, out_specs=out_specs, check_vma=False)
```
